512 devices in a mesh: seq: 64 (over x, z, core), grp: 2 (over y_hi), rep: 4 (over y_lo).
Axes of the slice: x: 4, y: 8 (y_hi: 2, y_lo: 4; y = y_hi * 4 + y_lo), z: 8, core: 2. Of those that a mesh axis runs over, the one named last changes fastest.
Arguments:
- queries: bfloat16 [8192, 4096], P(('rep', 'seq'), 'grp'), parts along dimension 0, may hold values from -6 to 6
- keys: bfloat16 [8192, 4096], P(('rep', 'seq'), 'grp'), parts along dimension 0, may hold values from -6 to 6
- values: bfloat16 [8192, 4096], P(('rep', 'seq'), 'grp'), parts along dimension 0, may hold values from -6 to 6
- q_gain: float32 [4096], P('grp'), may hold values from 0.1 to 1.9
- k_gain: float32 [4096], P('grp'), may hold values from 0.1 to 1.9
- clip_ids: int32 [8192], P(('rep', 'seq')), parts along dimension 0, may hold values from 0 to 3, never falling along the last dimension, each value on 1 to 1024 neighbouring positions
- features: bfloat16 [4, 128, 128, 384], P('rep', 'seq', 'grp'), parts along dimension 0, may hold values from -6 to 6
- frame_cache: bfloat16 [8, 128, 128, 384], P('rep', 'seq', 'grp'), parts along dimension 0, may hold values from -4 to 4
- feat_gain: float32 [384], replicated, may hold values from 0.1 to 1.9
- conv_weight: bfloat16 [10368, 384], P('seq'), may hold values from -0.0625 to 0.0625
Outputs:
- attended: bfloat16 [8192, 4096], P(('rep', 'seq'), 'grp'), parts along dimension 0
- decoded: bfloat16 [4, 128, 128, 384], P('rep', 'seq', 'grp'), parts along dimension 0
The draws below stay inside these ranges and needn't reach their ends.
There are 4 independent parts, one for each index of `rep`. The reference program is written for one: setup_inputs(seed, part) draws one part's arguments, and reference() takes and returns one part's arrays. A program takes and returns all parts, laid end to end along the dimension named above; an argument that names none is the same for every part. Nothing has to cross between parts.
All inputs are finite; a program needn't handle non-finite values.
Results may differ from the reference program's by a relative error of at most 0.0084.
Values may be sent and summed in bfloat16 or wider, within the bound.
No kernel may reach another device: no remote copies, remote signals or barrier semaphores. Data moves between devices by JAX's collectives and lax.ppermute only.
A program may use at most 64 MiB of HBM per device.

```python
import math
import jax
import jax.numpy as jnp
import numpy as np
from jax import lax

HEADS = 32
HEAD_DIM = 128
CH = 384
CLIPS = 4
FRAMES = 1
TOKENS = 2048
CLIP_MOST = 1024
ROWS_ALL = 128
COLS_ALL = 128


def draw_queries(key, part):
    key = jax.random.fold_in(key, 1)
    base = jax.random.normal(key, (TOKENS, HEADS * HEAD_DIM), jnp.float32)
    return jnp.clip(base, -6.0, 6.0).astype(jnp.bfloat16)


def draw_keys(key, part):
    key = jax.random.fold_in(key, 2)
    base = jax.random.normal(key, (TOKENS, HEADS * HEAD_DIM), jnp.float32)
    return jnp.clip(base, -6.0, 6.0).astype(jnp.bfloat16)


def levels(rng, dims, cuts, least, high):
    def one(dim, blocks):
        draws = jax.random.uniform(jax.random.fold_in(jax.random.fold_in(rng, 6), dim), (blocks,), jnp.float32, least / len(cuts), high / len(cuts))
        return jnp.repeat(jnp.exp(draws), dims[dim] // blocks).reshape((-1,) + (1,) * (len(dims) - dim - 1))

    loudness = one(*cuts[0])
    for cut in cuts[1:]:
        loudness = loudness * one(*cut)
    return loudness


def split_up(number_of, total, limit, skew):
    portions = [(1 << 20) // math.isqrt(grade ** skew) + 1 for grade in range(2, number_of + 1)]
    spare, given = total - limit - (number_of - 1), [1] * (number_of - 1)
    while spare > 0:
        candidates = [i for i in range(number_of - 1) if given[i] < limit]
        pool, left = sum([portions[i] for i in candidates]), spare
        for i in candidates:
            extra = min(limit - given[i], max(1, left * portions[i] // pool), spare)
            given[i] = given[i] + extra
            spare = spare - extra
    return np.array([limit] + given)


def uneven_parts(stream_key, amount, total, most, lean):
    if amount == 2:
        one = jax.random.randint(stream_key, (), max(1, total - most), min(most, total - 1) + 1)
        return jnp.stack([one, total - one])
    sizes = jnp.asarray(split_up(amount, total, most, lean), jnp.int32)
    couples = (amount - 1) // 2
    source_of, taker = sizes[1:1 + 2 * couples:2], sizes[2:2 + 2 * couples:2]
    margin = jnp.minimum(source_of - 1, most - taker)
    shifted = jax.random.randint(jax.random.fold_in(stream_key, 1), (couples,), 0, 1 << 20) % (margin + 1)
    sizes = sizes.at[1:1 + 2 * couples:2].set(source_of - shifted).at[2:2 + 2 * couples:2].set(taker + shifted)
    return sizes[jax.random.permutation(jax.random.fold_in(stream_key, 2), amount)]


def gaussian(key, dims, spread, most, pieces=(), held_as=jnp.bfloat16):
    drawn = jax.random.normal(key, dims, jnp.float32) * spread
    if len(pieces) > 0:
        drawn = levels(key, dims, pieces, -0.22, 0.18) * drawn
    return jnp.clip(drawn, min=-most, max=most).astype(held_as)


def setup_inputs(seed: int = 0, part: int = 0) -> dict:
    streams_of = jax.random.split(jax.random.key(seed), 11)
    part_splits = jax.random.split(jax.random.fold_in(streams_of[10], part), 11)
    return {
        "queries": draw_queries(jax.random.fold_in(jax.random.fold_in(streams_of[10], part), 71), part),
        "keys": draw_keys(jax.random.fold_in(jax.random.fold_in(streams_of[10], part), 71), part),
        "values": gaussian(part_splits[2], (TOKENS, HEADS * HEAD_DIM), 1.0, 6.0, ((0, 64), (1, 2))),
        "q_gain": jnp.clip(1.0 + 0.18 * jax.random.normal(streams_of[3], (HEADS * HEAD_DIM,), jnp.float32), 0.1, 1.9),
        "k_gain": jnp.clip(1.0 + 0.18 * jax.random.normal(streams_of[4], (HEADS * HEAD_DIM,), jnp.float32), 0.1, 1.9),
        "clip_ids": jnp.searchsorted(jnp.cumsum(uneven_parts(part_splits[5], CLIPS, TOKENS, CLIP_MOST, 1)), jnp.arange(TOKENS), side="right").astype(jnp.int32),
        "features": gaussian(part_splits[6], (FRAMES, ROWS_ALL, COLS_ALL, CH), 1.0, 6.0, ((1, 64), (2, 2))),
        "frame_cache": gaussian(part_splits[7], (2, ROWS_ALL, COLS_ALL, CH), 0.5, 4.0, ((1, 64), (2, 2))),
        "feat_gain": jnp.clip(1.0 + 0.18 * jax.random.normal(streams_of[8], (CH,), jnp.float32), 0.1, 1.9),
        "conv_weight": gaussian(streams_of[9], (27 * CH, CH), (27 * CH) ** -0.5, 0.0625, ((0, 64),)),
    }


epsilon = 1e-06

def rms_scale(raw, gain):
    values_f = raw.astype(jnp.float32)
    mean_sq = lax.optimization_barrier(jnp.mean(values_f * values_f, axis=-1, keepdims=True))
    return values_f * lax.rsqrt(mean_sq + epsilon) * gain

def reference(queries, keys, values, q_gain, k_gain, clip_ids, features, frame_cache, feat_gain, conv_weight):
    q_norm = rms_scale(queries, q_gain).astype(jnp.bfloat16)
    k_norm = rms_scale(keys, k_gain).astype(jnp.bfloat16)
    head_q = q_norm.reshape(TOKENS, HEADS, HEAD_DIM).transpose(1, 0, 2)
    head_k = k_norm.reshape(TOKENS, HEADS, HEAD_DIM).transpose(1, 0, 2)
    head_v = values.reshape(TOKENS, HEADS, HEAD_DIM).transpose(1, 0, 2)
    same_clip = clip_ids[:, None] == clip_ids[None, :]
    score_scale = 1.0 / HEAD_DIM ** 0.5

    def one_head(triple):
        query_h, key_h, value_h = triple
        scores = jnp.dot(query_h, key_h.T, preferred_element_type=jnp.float32) * score_scale
        scores = jnp.where(same_clip, scores, -1e+30)
        row_max = lax.optimization_barrier(jnp.max(scores, axis=-1, keepdims=True))
        probs = jnp.exp(scores - row_max)
        row_total = lax.optimization_barrier(jnp.sum(probs, axis=-1, keepdims=True))
        mixed_out = jnp.dot(probs.astype(jnp.bfloat16), value_h, preferred_element_type=jnp.float32)
        return (mixed_out / row_total).astype(jnp.bfloat16)
    per_head = lax.map(one_head, (head_q, head_k, head_v))
    attended = per_head.transpose(1, 0, 2).reshape(TOKENS, HEADS * HEAD_DIM)
    feat_float = features.astype(jnp.float32)
    activated = jax.nn.silu(rms_scale(features, feat_gain)).astype(jnp.bfloat16)
    stacked = jnp.concatenate([frame_cache, activated], axis=0)[None]
    kernel = conv_weight.reshape(3, 3, 3, CH, CH)
    convolved = lax.conv_general_dilated(stacked, kernel, (1, 1, 1), [(0, 0), (1, 1), (1, 1)], dimension_numbers=('NDHWC', 'DHWIO', 'NDHWC'), preferred_element_type=jnp.float32)[0]
    decoded = (feat_float + convolved).astype(jnp.bfloat16)
    return (attended, decoded)
```

```python
import functools
import math

import jax
import jax.numpy as jnp
from jax import lax
from jax.experimental import pallas as pl
from jax.experimental.pallas import tpu as pltpu
from jax.sharding import Mesh
from jax.sharding import PartitionSpec as P

HEADS = 32
HEAD_DIM = 128
CH = 384
WIDTH = HEADS * HEAD_DIM
EPS = 1e-06
SEQ = ("x", "z", "core")
HEAD_AXES = ("z", "core")
BF = jnp.bfloat16
F32 = jnp.float32
VMEM = pl.BlockSpec(memory_space=pltpu.VMEM)


def attention_kernel(tok, q_ref, own_ref, b_ref, c_ref, d_ref, qid_ref, out_ref):
    groups = q_ref.shape[0]
    count = groups * tok
    scale = 1.0 / math.sqrt(HEAD_DIM)
    q = q_ref[:, :tok, :].reshape(count, HEAD_DIM)
    keys, vals, ids = [], [], []
    for ref in (own_ref, b_ref, c_ref, d_ref):
        pairs = ref[: 2 * count, :].reshape(groups, 2 * tok, HEAD_DIM)
        keys.append(pairs[:, :tok].reshape(count, HEAD_DIM))
        vals.append(pairs[:, tok:].reshape(count, HEAD_DIM))
        rows = ref[2 * count : 2 * count + 16, :].astype(F32)
        ids.append(jnp.concatenate([rows[i : i + 1] for i in range(count // HEAD_DIM)], axis=1))
    step = 128
    for lo in range(0, count, step):
        q_id = qid_ref[lo : lo + step, :]
        scores = []
        for key, key_id in zip(keys, ids):
            s = lax.dot_general(
                q[lo : lo + step], key, (((1,), (1,)), ((), ())), preferred_element_type=F32
            )
            scores.append(jnp.where(q_id == key_id, s * scale, -1e30))
        top = functools.reduce(
            jnp.maximum, [jnp.max(s, axis=-1, keepdims=True) for s in scores]
        )
        total = jnp.zeros((step, 1), F32)
        mixed = jnp.zeros((step, HEAD_DIM), F32)
        for s, val in zip(scores, vals):
            probs = jnp.exp(s - top)
            total = total + jnp.sum(probs, axis=-1, keepdims=True)
            mixed = mixed + jnp.dot(probs.astype(BF), val, preferred_element_type=F32)
        out_ref[lo : lo + step, :] = (mixed / total).astype(BF)


SLOTS = 8


def conv_kernel(share, base_ref, slab_ref, own_ref, b_ref, c_ref, d_ref, out_ref, pad_ref, low_ref, high_ref):
    _, parts, _, high, cols, lanes = slab_ref.shape
    rows = high - 2
    cells = rows * cols
    half = SLOTS // 2
    pad_ref[...] = jnp.zeros_like(pad_ref)
    for p, ref in enumerate((own_ref, b_ref, c_ref, d_ref)):
        for j in range(SLOTS):
            pad_ref[j, :share, :128] = ref[j * share : (j + 1) * share, :]
            start = SLOTS * share + (j % half) * share
            pad_ref[j, :share, 128:] = ref[start : start + share, :]
        for part in range(parts):
            for side, total_ref in ((0, low_ref), (1, high_ref)):
                pieces = []
                for j in range(half):
                    tap = jnp.minimum(base_ref[p] + side * half + j, 26)
                    t, r, c = tap // 9, (tap // 3) % 3, tap % 3
                    pieces.append(
                        slab_ref[c, part, t, pl.ds(r, rows), :, :].reshape(cells, lanes)
                    )
                patches = jnp.concatenate(pieces, axis=1)
                weight = pad_ref[side * half : (side + 1) * half].reshape(half * lanes, 256)
                product = jnp.dot(patches, weight, preferred_element_type=F32)
                if p == 0:
                    total_ref[part] = product
                else:
                    total_ref[part] += product
    lane = lax.broadcasted_iota(jnp.int32, (cells // 2, 128), 1)
    for part in range(parts):
        low, top = low_ref[part], high_ref[part]
        out_ref[part, :cells, :] = (low[:, :128] + top[:, :128]).astype(BF)
        rest = low[:, 128:] + pltpu.roll(top[:, 128:], 64, axis=1)
        rest = jnp.where(lane < 64, rest[: cells // 2], pltpu.roll(rest[cells // 2 :], 64, axis=1))
        out_ref[part, cells:, :] = rest.astype(BF)


def ring(data, axis, by):
    count = lax.axis_size(axis)
    return lax.ppermute(data, axis, [(i, (i + by) % count) for i in range(count)])


def planes_of(data):
    count = lax.axis_size("x")
    return ring(data, "x", 1), ring(data, "x", count - 1), ring(data, "x", 2)


def exchange(data, axes):
    return lax.all_to_all(data, axes, split_axis=0, concat_axis=0, tiled=True)


def shards(
    queries, keys, values, q_gain, k_gain, clip_ids, features, frame_cache, feat_gain, conv_weight
):
    tok, local_cols = queries.shape
    heads = local_cols // HEAD_DIM
    planes = lax.axis_size("x")
    plane_tok = heads * tok
    deep, cores = lax.axis_size("z"), lax.axis_size("core")
    seq_count = planes * deep * cores
    me_x, me_core = lax.axis_index("x"), lax.axis_index("core")
    me_grp, me_rep = lax.axis_index("grp"), lax.axis_index("rep")
    parts = lax.axis_size("rep")
    order = jnp.stack([me_x, me_x - 1, me_x + 1, me_x + 2]) % planes

    q_f, k_f = queries.astype(F32), keys.astype(F32)
    sums = jnp.stack([jnp.sum(q_f * q_f, axis=-1), jnp.sum(k_f * k_f, axis=-1)])
    sums = sums + ring(sums, "grp", 1)

    lanes = 128
    share = CH // parts
    weight_rows = conv_weight.shape[0]
    first = (me_rep + 2 * me_core) % parts
    held = jnp.arange(48)[:, None]
    late = (me_core == 1) & (me_rep >= 2)
    source = jnp.where(
        held < 40,
        4 * (held + late.astype(jnp.int32)) + first,
        jnp.where((held == 40) & (first < 2), jnp.where(me_core == 1, first, 160 + first), -1),
    )
    pick = (source == jnp.arange(weight_rows)[None, :]).astype(BF)
    chosen = jnp.dot(pick, conv_weight, preferred_element_type=F32).astype(BF)
    halves = chosen.reshape(48, cores, CH // cores).transpose(1, 0, 2)
    last = halves[:, :, 128:]
    halves = jnp.concatenate(
        [halves[:, :, :128], jnp.concatenate([last[:, :24], last[:, 24:]], axis=2)], axis=1
    )
    sent_weight = jnp.broadcast_to(halves[None], (deep,) + halves.shape).reshape(-1, 72, 128)
    plane_weight = exchange(sent_weight, HEAD_AXES)

    scales = lax.rsqrt(sums / WIDTH + EPS)
    q_norm = (q_f * scales[0][:, None] * q_gain).astype(BF)
    k_norm = (k_f * scales[1][:, None] * k_gain).astype(BF)
    id_row = jnp.pad(clip_ids.astype(BF)[None, :], ((0, 7), (0, HEAD_DIM - tok)))

    def by_head(data):
        return data.reshape(tok, heads, HEAD_DIM).transpose(1, 0, 2)

    payload = jnp.concatenate(
        [
            by_head(q_norm),
            by_head(k_norm),
            by_head(values),
            jnp.broadcast_to(id_row[None], (heads,) + id_row.shape),
        ],
        axis=1,
    )
    got = exchange(payload, HEAD_AXES)
    ids_got = got[:, 3 * tok, :tok].reshape(-1)
    id_block = jnp.pad(ids_got.reshape(-1, HEAD_DIM), ((0, 16 - plane_tok // HEAD_DIM), (0, 0)))
    key_vals = jnp.concatenate(
        [got[:, tok : 3 * tok, :].reshape(2 * plane_tok, HEAD_DIM), id_block], axis=0
    )

    slot = jnp.arange(deep * cores * 48)
    spot, item = slot // 48, slot % 48
    target = 81 * (spot // cores) + jnp.where(item == 40, 40, item + 41 * (spot % cores))
    target = jnp.where(item > 40, -1, target + (648 * me_x) % share)
    place = (jnp.arange(SLOTS * share)[:, None] == target[None, :]).astype(BF)
    place = place.reshape(SLOTS * share, deep * cores, 48)
    main = plane_weight[:, :48, :]
    rest = plane_weight[:, 48:, :]

    def placed_rows(at, data):
        return lax.dot_general(
            at, data, (((1, 2), (0, 1)), ((), ())), preferred_element_type=F32
        ).astype(BF)

    last_cols = (
        placed_rows(place[:, :, :24], rest)[:, :64] + placed_rows(place[:, :, 24:], rest)[:, 64:]
    )
    split = SLOTS * share // 2
    my_weight = jnp.concatenate(
        [
            placed_rows(place, main),
            jnp.concatenate([last_cols[:split], last_cols[split:]], axis=1),
        ],
        axis=0,
    )
    weights = (my_weight,) + planes_of(my_weight)
    taps = (27 * order) // planes

    others = planes_of(key_vals)
    head_out = pl.pallas_call(
        functools.partial(attention_kernel, tok),
        out_shape=jax.ShapeDtypeStruct((plane_tok, HEAD_DIM), BF),
        in_specs=[VMEM] * 6,
        out_specs=VMEM,
        compiler_params=pltpu.CompilerParams(vmem_limit_bytes=40 << 20),
        cost_estimate=pl.CostEstimate(
            flops=2 * 2 * plane_tok * plane_tok * planes * HEAD_DIM,
            bytes_accessed=planes * plane_tok * HEAD_DIM * 4,
            transcendentals=plane_tok * plane_tok * planes,
        ),
        name="attention",
    )(got, key_vals, *others, ids_got.astype(F32)[:, None])
    returned = exchange(head_out.reshape(heads, tok, HEAD_DIM), HEAD_AXES)
    attended = returned.transpose(1, 0, 2).reshape(tok, local_cols)

    frames, tile_rows, tile_cols, _ = features.shape
    feat_f = features.astype(F32)
    scaled = (
        feat_f
        * lax.rsqrt(jnp.mean(feat_f * feat_f, axis=-1, keepdims=True) + EPS)
        * feat_gain
    )
    activated = jax.nn.silu(scaled).astype(BF)
    stacked = jnp.concatenate([frame_cache, activated], axis=0).reshape(-1, CH)
    lane = jnp.arange(parts * lanes)
    chan = jnp.where(lane % lanes < share, parts * (lane % lanes) + lane // lanes, -1)
    sort = (jnp.arange(CH)[:, None] == chan[None, :]).astype(BF)
    sorted_cells = jnp.dot(stacked, sort, preferred_element_type=F32).astype(BF)
    outgoing = sorted_cells.reshape(-1, parts, lanes).transpose(1, 0, 2)
    cells = exchange(outgoing, "rep").reshape(parts, 3, tile_rows, tile_cols, lanes)
    is_upper = me_core == 0
    outer = jnp.where(is_upper, cells[:, :, :1], cells[:, :, -1:])
    pairs = [(s, s - 1 if s % 2 == 0 else s + 1) for s in range(1, seq_count - 1)]
    beyond = lax.ppermute(outer, SEQ, pairs)
    mine = jnp.where(
        is_upper,
        jnp.concatenate([beyond, cells], axis=2),
        jnp.concatenate([cells, beyond], axis=2),
    )
    theirs = ring(mine, "core", 1)
    tall = jnp.where(
        is_upper,
        jnp.concatenate([mine, theirs], axis=2),
        jnp.concatenate([theirs, mine], axis=2),
    )
    is_left = me_grp == 0
    edge = jnp.where(is_left, tall[:, :, :, -1:], tall[:, :, :, :1])
    beside = ring(edge, "grp", 1)
    nothing = jnp.zeros_like(beside)
    wide = jnp.concatenate(
        [jnp.where(is_left, nothing, beside), tall, jnp.where(is_left, beside, nothing)], axis=3
    )
    slab = jnp.stack([wide[:, :, :, c : c + tile_cols] for c in range(3)])
    chip_cells = cores * tile_rows * tile_cols
    partial = pl.pallas_call(
        functools.partial(conv_kernel, share),
        out_shape=jax.ShapeDtypeStruct((parts, chip_cells + chip_cells // 2, 128), BF),
        in_specs=[pl.BlockSpec(memory_space=pltpu.SMEM)] + [VMEM] * 5,
        out_specs=VMEM,
        scratch_shapes=[
            pltpu.VMEM((SLOTS, lanes, 256), BF),
            pltpu.VMEM((parts, chip_cells, 256), F32),
            pltpu.VMEM((parts, chip_cells, 256), F32),
        ],
        compiler_params=pltpu.CompilerParams(vmem_limit_bytes=48 << 20),
        cost_estimate=pl.CostEstimate(
            flops=2 * parts * chip_cells * 32 * lanes * 256,
            bytes_accessed=27 * lanes * CH,
            transcendentals=0,
        ),
        name="convolution",
    )(taps.astype(jnp.int32), slab, *weights)
    sums_back = jnp.sum(exchange(partial, "rep").astype(F32), axis=0)
    tile_cells = tile_rows * tile_cols
    main_cols = sums_back[:chip_cells].reshape(cores, tile_cells, 128)
    last_cols = sums_back[chip_cells:].reshape(tile_cells, cores, 64).transpose(1, 0, 2)
    both = jnp.concatenate([main_cols, last_cols], axis=2)
    keep = jnp.where(is_upper, both[0], both[1])
    give = jnp.where(is_upper, both[1], both[0]).astype(BF)
    take = ring(give, "core", 1).astype(F32)
    convolved = jnp.where(
        is_upper,
        jnp.concatenate([keep, take], axis=1),
        jnp.concatenate([take, keep], axis=1),
    ).reshape(features.shape)
    decoded = (feat_f + convolved).astype(BF)
    return (attended, decoded)


def solution(mesh):
    grid = Mesh(
        mesh.devices.reshape((4, 8, 2) + mesh.devices.shape[1:]), ("x", "z", "core", "grp", "rep")
    )
    tokens = P(("rep",) + SEQ, "grp")
    image = P("rep", SEQ, "grp", None)
    placed = (
        tokens,
        tokens,
        tokens,
        P("grp"),
        P("grp"),
        P(("rep",) + SEQ),
        image,
        image,
        P(),
        P(SEQ, None),
    )
    return jax.shard_map(
        shards, mesh=grid, in_specs=placed, out_specs=(tokens, image), check_vma=False
    )
```

```python
import functools
import math

import jax
import jax.numpy as jnp
from jax import lax
from jax.experimental import pallas as pl
from jax.experimental.pallas import tpu as pltpu
from jax.sharding import Mesh
from jax.sharding import PartitionSpec as P

HEADS = 32
HEAD_DIM = 128
CH = 384
WIDTH = HEADS * HEAD_DIM
EPS = 1e-06
X = ("xh", "xl")
SEQ = ("xh", "xl", "z", "core")
HEAD_AXES = ("xl", "z")
BF = jnp.bfloat16
F32 = jnp.float32
VMEM = pl.BlockSpec(memory_space=pltpu.VMEM)


def attention_kernel(tok, q_ref, pair_ref, other_ref, qid_ref, out_ref):
    groups = q_ref.shape[0]
    count = groups * tok
    scale = 1.0 / math.sqrt(HEAD_DIM)
    q = q_ref[:, :tok, :].reshape(count, HEAD_DIM)
    keys, vals, ids = [], [], []
    for ref in (pair_ref.at[0], pair_ref.at[1], other_ref.at[0], other_ref.at[1]):
        pairs = ref[: 2 * count, :].reshape(groups, 2 * tok, HEAD_DIM)
        keys.append(pairs[:, :tok].reshape(count, HEAD_DIM))
        vals.append(pairs[:, tok:].reshape(count, HEAD_DIM))
        rows = ref[2 * count : 2 * count + 16, :].astype(F32)
        ids.append(jnp.concatenate([rows[i : i + 1] for i in range(count // HEAD_DIM)], axis=1))
    step = 128
    for lo in range(0, count, step):
        q_id = qid_ref[lo : lo + step, :]
        scores = []
        for key, key_id in zip(keys, ids):
            s = lax.dot_general(
                q[lo : lo + step], key, (((1,), (1,)), ((), ())), preferred_element_type=F32
            )
            scores.append(jnp.where(q_id == key_id, s * scale, -1e30))
        top = functools.reduce(
            jnp.maximum, [jnp.max(s, axis=-1, keepdims=True) for s in scores]
        )
        total = jnp.zeros((step, 1), F32)
        mixed = jnp.zeros((step, HEAD_DIM), F32)
        for s, val in zip(scores, vals):
            probs = jnp.exp(s - top)
            total = total + jnp.sum(probs, axis=-1, keepdims=True)
            mixed = mixed + jnp.dot(probs.astype(BF), val, preferred_element_type=F32)
        out_ref[lo : lo + step, :] = (mixed / total).astype(BF)


SLOTS = 8


def conv_kernel(share, base_ref, slab_ref, own_ref, b_ref, c_ref, d_ref, out_ref, pad_ref, total_ref):
    _, _, high, cols, lanes = slab_ref.shape
    rows = high - 2
    step = 2
    pad_ref[...] = jnp.zeros_like(pad_ref)
    for p, ref in enumerate((own_ref, b_ref, c_ref, d_ref)):
        for j in range(SLOTS):
            pad_ref[j, :share, :] = ref[j * share : (j + 1) * share, :]
        for lo in range(0, rows, step):
            pieces = []
            for j in range(SLOTS):
                tap = jnp.minimum(base_ref[p] + j, 26)
                t, r, c = tap // 9, (tap // 3) % 3, tap % 3
                pieces.append(
                    slab_ref[c, t, pl.ds(r + lo, step), :, :].reshape(step * cols, lanes)
                )
            product = jnp.dot(
                jnp.concatenate(pieces, axis=1),
                pad_ref[...].reshape(SLOTS * lanes, CH),
                preferred_element_type=F32,
            )
            at = slice(lo * cols, (lo + step) * cols)
            if p == 0:
                total_ref[at, :] = product
            else:
                total_ref[at, :] += product
    out_ref[...] = total_ref[...].astype(BF)


def ring(data, axis, by):
    count = lax.axis_size(axis)
    return lax.ppermute(data, axis, [(i, (i + by) % count) for i in range(count)])


def three_parts(total):
    high = lax.reduce_precision(total, 8, 7)
    mid = lax.reduce_precision(total - high, 8, 7)
    return jnp.stack([high, mid, (total - high) - mid]).astype(BF)


def planes_of(data):
    count = lax.axis_size(X)
    return ring(data, X, 1), ring(data, X, count - 1), ring(data, X, 2)


def exchange(data, axes):
    return lax.all_to_all(data, axes, split_axis=0, concat_axis=0, tiled=True)


def shards(
    queries, keys, values, q_gain, k_gain, clip_ids, features, frame_cache, feat_gain, conv_weight
):
    tok, local_cols = queries.shape
    heads = local_cols // HEAD_DIM
    planes = lax.axis_size(X)
    plane_tok = heads * tok
    deep, cores = lax.axis_size("z"), lax.axis_size("core")
    seq_count = planes * deep * cores
    me_x, me_core = lax.axis_index(X), lax.axis_index("core")
    me_grp = lax.axis_index("grp")
    order = jnp.stack([me_x, me_x - 1, me_x + 1, me_x + 2]) % planes

    lanes = 128
    classes = 2 * cores
    share = CH // classes
    weight_rows = conv_weight.shape[0]
    held = jnp.arange(48)[:, None]

    def rows_of(kind):
        first = (kind + 2 * me_core) % classes
        late = (me_core == 1) & (kind >= 2)
        source = jnp.where(
            held < 40,
            classes * (held + late.astype(jnp.int32)) + first,
            jnp.where((held == 40) & (first < 2), jnp.where(me_core == 1, first, 160 + first), -1),
        )
        return source == jnp.arange(weight_rows)[None, :]

    pick = jnp.concatenate([rows_of(2 * me_grp + c) for c in range(cores)], axis=0).astype(BF)
    chosen = jnp.dot(pick, conv_weight, preferred_element_type=F32).astype(BF)
    chosen = chosen.reshape(1, cores, 48, CH)
    sent_weight = jnp.broadcast_to(chosen, (deep,) + chosen.shape[1:]).reshape(-1, 48, CH)
    plane_weight = exchange(sent_weight, ("z", "core"))

    q_f, k_f = queries.astype(F32), keys.astype(F32)
    sums = jnp.stack([jnp.sum(q_f * q_f, axis=-1), jnp.sum(k_f * k_f, axis=-1)])
    frames, tile_rows, tile_cols, _ = features.shape
    feat_f = features.astype(F32)
    scaled = (
        feat_f
        * lax.rsqrt(jnp.mean(feat_f * feat_f, axis=-1, keepdims=True) + EPS)
        * feat_gain
    )
    activated = jax.nn.silu(scaled).astype(BF)
    stacked = jnp.concatenate([frame_cache, activated], axis=0).reshape(-1, CH)
    lane = jnp.arange(classes * lanes)
    slot = lane // lanes
    kind = 2 * ((me_grp + slot // 2) % 2) + slot % 2
    chan = jnp.where(lane % lanes < share, classes * (lane % lanes) + kind, -1)
    sort = (jnp.arange(CH)[:, None] == chan[None, :]).astype(BF)
    sorted_cells = jnp.dot(stacked, sort, preferred_element_type=F32).astype(BF)
    sorted_cells = sorted_cells.reshape(-1, classes, lanes).transpose(1, 0, 2)
    count = sorted_cells.shape[1]
    parts_of = jnp.pad(three_parts(sums).reshape(-1, tok), ((0, 10), (0, lanes - tok)))
    outgoing = jnp.concatenate([sorted_cells[2:].reshape(2 * count, lanes), parts_of], axis=0)
    incoming = ring(outgoing, "grp", 1)
    theirs = incoming[2 * count : 2 * count + 6, :tok].astype(F32).reshape(3, 2, tok)
    sums = sums + ((theirs[0] + theirs[1]) + theirs[2])
    mine = sorted_cells[:2].reshape(2, 3, tile_rows, tile_cols, lanes)
    other = incoming[: 2 * count].reshape(2, 3, tile_rows, tile_cols, lanes)
    is_left, is_upper = me_grp == 0, me_core == 0
    wide = jnp.where(
        is_left,
        jnp.concatenate([mine, other], axis=3),
        jnp.concatenate([other, mine], axis=3),
    )
    outer = jnp.where(is_upper, wide[:, :, :1], wide[:, :, -1:])
    pairs = [(s, s - 1 if s % 2 == 0 else s + 1) for s in range(1, seq_count - 1)]
    beyond = lax.ppermute(outer, SEQ, pairs)
    held_rows = jnp.where(
        is_upper,
        jnp.concatenate([beyond, wide], axis=2),
        jnp.concatenate([wide, beyond], axis=2),
    )
    keep = jnp.where(is_upper, held_rows[0], held_rows[1])
    give = jnp.where(is_upper, held_rows[1], held_rows[0])
    take = ring(give, "core", 1)
    tall = jnp.where(
        is_upper,
        jnp.concatenate([keep, take], axis=1),
        jnp.concatenate([take, keep], axis=1),
    )
    full_cols = 2 * tile_cols
    padded = jnp.pad(tall, ((0, 0), (0, 0), (1, 1), (0, 0)))
    slab = jnp.stack([padded[:, :, c : c + full_cols] for c in range(3)])

    scales = lax.rsqrt(sums / WIDTH + EPS)
    q_norm = (q_f * scales[0][:, None] * q_gain).astype(BF)
    k_norm = (k_f * scales[1][:, None] * k_gain).astype(BF)
    id_row = jnp.pad(clip_ids.astype(BF)[None, :], ((0, 7), (0, HEAD_DIM - tok)))

    def by_head(data):
        return data.reshape(tok, heads, HEAD_DIM).transpose(1, 0, 2)

    payload = jnp.concatenate(
        [
            by_head(q_norm),
            by_head(k_norm),
            by_head(values),
            jnp.broadcast_to(id_row[None], (heads,) + id_row.shape),
        ],
        axis=1,
    )
    got = exchange(payload, HEAD_AXES)
    ids_got = got[:, 3 * tok, :tok].reshape(-1)
    id_block = jnp.pad(ids_got.reshape(-1, HEAD_DIM), ((0, 16 - plane_tok // HEAD_DIM), (0, 0)))
    key_vals = jnp.concatenate(
        [got[:, tok : 3 * tok, :].reshape(2 * plane_tok, HEAD_DIM), id_block], axis=0
    )

    spot_item = jnp.arange(deep * cores * 48)
    spot, item = spot_item // 48, spot_item % 48
    target = 81 * (spot // cores) + jnp.where(item == 40, 40, item + 41 * (spot % cores))
    target = jnp.where(item > 40, -1, target + (648 * me_x) % share)
    place = (jnp.arange(SLOTS * share)[:, None] == target[None, :]).astype(BF)
    my_weight = jnp.dot(
        place, plane_weight.reshape(-1, CH), preferred_element_type=F32
    ).astype(BF)
    weights = (my_weight,) + planes_of(my_weight)
    taps = (27 * order) // planes

    pair = jnp.stack([key_vals, ring(key_vals, "xh", 1)])
    other_pair = ring(pair, "core", 1)
    head_out = pl.pallas_call(
        functools.partial(attention_kernel, tok),
        out_shape=jax.ShapeDtypeStruct((plane_tok, HEAD_DIM), BF),
        in_specs=[VMEM] * 4,
        out_specs=VMEM,
        compiler_params=pltpu.CompilerParams(vmem_limit_bytes=40 << 20),
        cost_estimate=pl.CostEstimate(
            flops=2 * 2 * plane_tok * plane_tok * planes * HEAD_DIM,
            bytes_accessed=planes * plane_tok * HEAD_DIM * 4,
            transcendentals=plane_tok * plane_tok * planes,
        ),
        name="attention",
    )(got, pair, other_pair, ids_got.astype(F32)[:, None])
    returned = exchange(head_out.reshape(heads, tok, HEAD_DIM), HEAD_AXES)
    attended = returned.transpose(1, 0, 2).reshape(tok, local_cols)

    cells = cores * tile_rows * full_cols
    partial = pl.pallas_call(
        functools.partial(conv_kernel, share),
        out_shape=jax.ShapeDtypeStruct((cells, CH), BF),
        in_specs=[pl.BlockSpec(memory_space=pltpu.SMEM)] + [VMEM] * 5,
        out_specs=VMEM,
        scratch_shapes=[
            pltpu.VMEM((SLOTS, lanes, CH), BF),
            pltpu.VMEM((cells, CH), F32),
        ],
        compiler_params=pltpu.CompilerParams(vmem_limit_bytes=48 << 20),
        cost_estimate=pl.CostEstimate(
            flops=2 * cells * planes * SLOTS * lanes * CH,
            bytes_accessed=planes * SLOTS * share * CH * 2,
            transcendentals=0,
        ),
        name="convolution",
    )(taps.astype(jnp.int32), slab, *weights)
    by_core = partial.reshape(cores, tile_rows, 2, tile_cols, CH)
    keep = jnp.where(is_upper, by_core[0], by_core[1]).astype(F32)
    give = jnp.where(is_upper, by_core[1], by_core[0])
    by_half = keep + ring(give, "core", 1).astype(F32)
    keep = jnp.where(is_left, by_half[:, 0], by_half[:, 1])
    give = jnp.where(is_left, by_half[:, 1], by_half[:, 0]).astype(BF)
    convolved = keep + ring(give, "grp", 1).astype(F32)
    decoded = (feat_f + convolved.reshape(features.shape)).astype(BF)
    return (attended, decoded)


def solution(mesh):
    grid = Mesh(
        mesh.devices.reshape((2, 2, 8, 2) + mesh.devices.shape[1:]),
        ("xh", "xl", "z", "core", "grp", "rep"),
    )
    tokens = P(("rep",) + SEQ, "grp")
    image = P("rep", SEQ, "grp", None)
    placed = (
        tokens,
        tokens,
        tokens,
        P("grp"),
        P("grp"),
        P(("rep",) + SEQ),
        image,
        image,
        P(),
        P(SEQ, None),
    )
    return jax.shard_map(
        shards, mesh=grid, in_specs=placed, out_specs=(tokens, image), check_vma=False
    )
```

```python
import functools
import math

import jax
import jax.numpy as jnp
from jax import lax
from jax.experimental import pallas as pl
from jax.experimental.pallas import tpu as pltpu
from jax.sharding import Mesh
from jax.sharding import PartitionSpec as P

HEADS = 32
HEAD_DIM = 128
CH = 384
WIDTH = HEADS * HEAD_DIM
EPS = 1e-06
X = ("xh", "xl")
SEQ = ("xh", "xl", "z", "core")
HEAD_AXES = ("xl", "z")
BF = jnp.bfloat16
F32 = jnp.float32
VMEM = pl.BlockSpec(memory_space=pltpu.VMEM)


def attend(tok, q_ref, blocks, qid_ref, out_ref):
    groups = q_ref.shape[0]
    count = groups * tok
    scale = 1.0 / math.sqrt(HEAD_DIM)
    q = q_ref[:, :tok, :].reshape(count, HEAD_DIM)
    keys, vals, ids = [], [], []
    for ref in blocks:
        pairs = ref[: 2 * count, :].reshape(groups, 2 * tok, HEAD_DIM)
        keys.append(pairs[:, :tok].reshape(count, HEAD_DIM))
        vals.append(pairs[:, tok:].reshape(count, HEAD_DIM))
        rows = ref[2 * count : 2 * count + 16, :].astype(F32)
        ids.append(jnp.concatenate([rows[i : i + 1] for i in range(count // HEAD_DIM)], axis=1))
    step = 128
    for lo in range(0, count, step):
        q_id = qid_ref[lo : lo + step, :]
        scores = []
        for key, key_id in zip(keys, ids):
            s = lax.dot_general(
                q[lo : lo + step], key, (((1,), (1,)), ((), ())), preferred_element_type=F32
            )
            scores.append(jnp.where(q_id == key_id, s * scale, -1e30))
        top = functools.reduce(
            jnp.maximum, [jnp.max(s, axis=-1, keepdims=True) for s in scores]
        )
        total = jnp.zeros((step, 1), F32)
        mixed = jnp.zeros((step, HEAD_DIM), F32)
        for s, val in zip(scores, vals):
            probs = jnp.exp(s - top)
            total = total + jnp.sum(probs, axis=-1, keepdims=True)
            mixed = mixed + jnp.dot(probs.astype(BF), val, preferred_element_type=F32)
        out_ref[lo : lo + step, :] = (mixed / total).astype(BF)


def lay_out(core, left, cells_ref, halo_ref, slab_ref):
    _, parts, frames, _, cols, lanes = slab_ref.shape
    at = lax.broadcasted_iota(jnp.int32, (cols, lanes), 0)

    def put(part, t, row, cells, beside):
        wide = cells.astype(F32)
        before = jnp.where(at == 0, beside * left, pltpu.roll(wide, 1, axis=0))
        after = jnp.where(at == cols - 1, beside * (1.0 - left), pltpu.roll(wide, cols - 1, axis=0))
        slab_ref[0, part, t, row] = before.astype(BF)
        slab_ref[1, part, t, row] = cells
        slab_ref[2, part, t, row] = after.astype(BF)

    def one_part(part, _):
        base = pl.multiple_of(part * (2 * frames * cols + 16), 16)
        beside = cells_ref[pl.ds(base + 2 * frames * cols, 16), :].astype(F32)
        halo_base = pl.multiple_of(part * (frames * cols + 16), 16)
        beyond = halo_ref[pl.ds(halo_base + frames * cols, 16), :].astype(F32)
        for t in range(frames):
            for r in range(2):
                k = 2 * t + r
                cells = cells_ref[pl.ds(base + k * cols, cols), :]
                put(part, t, 1 + 2 * core + r, cells, beside[k : k + 1])
            put(part, t, 5 * core, halo_ref[pl.ds(halo_base + t * cols, cols), :], beyond[t : t + 1])
        return 0

    lax.fori_loop(0, parts, one_part, 0)


SLOTS = 8


def convolve(share, taps, slab_ref, planes, out_ref, pad_ref, low_ref, high_ref):
    _, parts, _, high, cols, lanes = slab_ref.shape
    rows = high - 2
    cells = rows * cols
    half = SLOTS // 2
    pad_ref[...] = jnp.zeros_like(pad_ref)
    for p, ref in enumerate(planes):
        for j in range(SLOTS):
            pad_ref[j, :share, :128] = ref[j * share : (j + 1) * share, :]
            start = SLOTS * share + (j % half) * share
            pad_ref[j, :share, 128:] = ref[start : start + share, :]
        for part in range(parts):
            for side, total_ref in ((0, low_ref), (1, high_ref)):
                pieces = []
                for j in range(half):
                    tap = jnp.minimum(taps(p) + side * half + j, 26)
                    t, r, c = tap // 9, (tap // 3) % 3, tap % 3
                    pieces.append(
                        slab_ref[c, part, t, pl.ds(r, rows), :, :].reshape(cells, lanes)
                    )
                patches = jnp.concatenate(pieces, axis=1)
                weight = pad_ref[side * half : (side + 1) * half].reshape(half * lanes, 256)
                product = jnp.dot(patches, weight, preferred_element_type=F32)
                if p == 0:
                    total_ref[part] = product
                else:
                    total_ref[part] += product
    lane = lax.broadcasted_iota(jnp.int32, (cells // 2, 128), 1)
    for part in range(parts):
        low, top = low_ref[part], high_ref[part]
        out_ref[part, :cells, :] = (low[:, :128] + top[:, :128]).astype(BF)
        rest = low[:, 128:] + pltpu.roll(top[:, 128:], 64, axis=1)
        rest = jnp.where(lane < 64, rest[: cells // 2], pltpu.roll(rest[cells // 2 :], 64, axis=1))
        out_ref[part, cells:, :] = rest.astype(BF)


def attention_kernel(tok, block, q_ref, mine_ref, theirs_ref, qid_ref, out_ref):
    blocks = [r.at[pl.ds(i * block, block)] for r in (mine_ref, theirs_ref) for i in range(2)]
    attend(tok, q_ref, blocks, qid_ref, out_ref)


def conv_kernel(share, sizes, place_ref, mine_ref, theirs_ref, *refs):
    *planes, conv_ref, slab_ref, pad_ref, low_ref, high_ref = refs
    block, cells, halo = sizes
    core, left = place_ref[0], place_ref[1].astype(F32)
    for own, ref in ((core, mine_ref), (1 - core, theirs_ref)):
        lay_out(
            own, left, ref.at[pl.ds(2 * block, cells)], ref.at[pl.ds(2 * block + cells, halo)], slab_ref
        )
    convolve(share, lambda p: place_ref[2 + p], slab_ref, planes, conv_ref, pad_ref, low_ref, high_ref)


def activate(cells, gain):
    cells = cells.astype(F32)
    scale = lax.rsqrt(jnp.mean(cells * cells, axis=-1, keepdims=True) + EPS)
    return jax.nn.silu(cells * scale * gain).astype(BF)


def three_parts(total):
    high = lax.reduce_precision(total, 8, 7)
    mid = lax.reduce_precision(total - high, 8, 7)
    return jnp.stack([high, mid, (total - high) - mid]).astype(BF)


def ring(data, axis, by):
    count = lax.axis_size(axis)
    return lax.ppermute(data, axis, [(i, (i + by) % count) for i in range(count)])


def planes_of(data):
    count = lax.axis_size(X)
    return ring(data, X, 1), ring(data, X, count - 1), ring(data, X, 2)


def exchange(data, axes):
    return lax.all_to_all(data, axes, split_axis=0, concat_axis=0, tiled=True)


def shards(
    queries, keys, values, q_gain, k_gain, clip_ids, features, frame_cache, feat_gain, conv_weight
):
    tok, local_cols = queries.shape
    heads = local_cols // HEAD_DIM
    planes = lax.axis_size(X)
    plane_tok = heads * tok
    deep, cores = lax.axis_size("z"), lax.axis_size("core")
    seq_count = planes * deep * cores
    me_x, me_core = lax.axis_index(X), lax.axis_index("core")
    me_grp, me_rep = lax.axis_index("grp"), lax.axis_index("rep")
    parts = lax.axis_size("rep")
    order = jnp.stack([me_x, me_x - 1, me_x + 1, me_x + 2]) % planes

    q_f, k_f = queries.astype(F32), keys.astype(F32)
    sums = jnp.stack([jnp.sum(q_f * q_f, axis=-1), jnp.sum(k_f * k_f, axis=-1)])
    lanes = 128
    frames, tile_rows, tile_cols, _ = features.shape
    is_left, is_upper = me_grp == 0, me_core == 0
    raw_edge = jnp.concatenate(
        [
            jnp.where(is_left, frame_cache[:, :, -1], frame_cache[:, :, 0]),
            jnp.where(is_left, features[:, :, -1], features[:, :, 0]),
        ]
    )
    edge_count = raw_edge.shape[0] * raw_edge.shape[1]
    first_out = jnp.concatenate(
        [
            jnp.pad(three_parts(sums).reshape(6, tok), ((0, 0), (0, lanes - tok))),
            raw_edge.reshape(-1, lanes),
        ]
    )
    first_in = ring(first_out, "grp", 1)
    theirs = first_in[:6, :tok].astype(F32).reshape(3, 2, tok)
    sums = sums + ((theirs[0] + theirs[1]) + theirs[2])
    beside = first_in[6:].reshape(edge_count, CH)

    share = CH // parts
    weight_rows = conv_weight.shape[0]
    first = (me_rep + 2 * me_core) % parts
    held = jnp.arange(48)[:, None]
    late = (me_core == 1) & (me_rep >= 2)
    source = jnp.where(
        held < 40,
        4 * (held + late.astype(jnp.int32)) + first,
        jnp.where((held == 40) & (first < 2), jnp.where(me_core == 1, first, 160 + first), -1),
    )
    pick = (source == jnp.arange(weight_rows)[None, :]).astype(BF)
    chosen = jnp.dot(pick, conv_weight, preferred_element_type=F32).astype(BF)
    halves = chosen.reshape(48, cores, CH // cores).transpose(1, 0, 2)
    last = halves[:, :, 128:]
    halves = jnp.concatenate(
        [halves[:, :, :128], jnp.concatenate([last[:, :24], last[:, 24:]], axis=2)], axis=1
    )
    sent_weight = jnp.broadcast_to(halves[None], (deep,) + halves.shape).reshape(-1, 72, 128)
    plane_weight = exchange(sent_weight, ("z", "core"))

    scales = lax.rsqrt(sums / WIDTH + EPS)
    q_norm = (q_f * scales[0][:, None] * q_gain).astype(BF)
    k_norm = (k_f * scales[1][:, None] * k_gain).astype(BF)
    id_row = jnp.pad(clip_ids.astype(BF)[None, :], ((0, 7), (0, HEAD_DIM - tok)))

    def by_head(data):
        return data.reshape(tok, heads, HEAD_DIM).transpose(1, 0, 2)

    payload = jnp.concatenate(
        [
            by_head(q_norm),
            by_head(k_norm),
            by_head(values),
            jnp.broadcast_to(id_row[None], (heads,) + id_row.shape),
        ],
        axis=1,
    )
    got = exchange(payload, HEAD_AXES)
    slot = jnp.arange(deep * cores * 48)
    spot, item = slot // 48, slot % 48
    target = 81 * (spot // cores) + jnp.where(item == 40, 40, item + 41 * (spot % cores))
    target = jnp.where(item > 40, -1, target + (648 * me_x) % share)
    place = (jnp.arange(SLOTS * share)[:, None] == target[None, :]).astype(BF)
    place = place.reshape(SLOTS * share, deep * cores, 48)
    main = plane_weight[:, :48, :]
    rest = plane_weight[:, 48:, :]

    def placed_rows(at, data):
        return lax.dot_general(
            at, data, (((1, 2), (0, 1)), ((), ())), preferred_element_type=F32
        ).astype(BF)

    last_cols = (
        placed_rows(place[:, :, :24], rest)[:, :64] + placed_rows(place[:, :, 24:], rest)[:, 64:]
    )
    split = SLOTS * share // 2
    my_weight = jnp.concatenate(
        [
            placed_rows(place, main),
            jnp.concatenate([last_cols[:split], last_cols[split:]], axis=1),
        ],
        axis=0,
    )
    weights = (my_weight,) + planes_of(my_weight)
    taps = (27 * order) // planes
    got, *near = lax.optimization_barrier((got,) + weights[1:3])
    weights = weights[:1] + tuple(near) + weights[3:]

    feat_f = features.astype(F32)
    stacked = jnp.concatenate([frame_cache, activate(features, feat_gain)], axis=0)
    lane = jnp.arange(parts * lanes)
    chan = jnp.where(
        lane % lanes < share, parts * (lane % lanes) + (me_rep + lane // lanes) % parts, -1
    )
    sort = (jnp.arange(CH)[:, None] == chan[None, :]).astype(BF)

    def by_class(data):
        data = jnp.dot(data, sort, preferred_element_type=F32).astype(BF)
        return data.reshape(-1, parts, lanes).transpose(1, 0, 2)

    beside = jnp.concatenate([beside[:-2], activate(beside[-2:], feat_gain)])
    beside = jnp.pad(beside, ((0, 16 - edge_count), (0, 0)))
    outgoing = jnp.concatenate([by_class(stacked.reshape(-1, CH)), by_class(beside)], axis=1)
    cells = jnp.stack([outgoing[0]] + [ring(outgoing[by], "rep", by) for by in range(1, parts)])
    main = cells[:, : 6 * tile_cols].reshape(parts, 3, tile_rows, tile_cols, lanes)
    ends = cells[:, 6 * tile_cols : 6 * tile_cols + 6].reshape(parts, 3, tile_rows, lanes)
    outer = jnp.where(is_upper, main[:, :, 0], main[:, :, -1]).reshape(parts, -1, lanes)
    outer_ends = jnp.where(is_upper, ends[:, :, 0], ends[:, :, -1])
    outer = jnp.concatenate([outer, jnp.pad(outer_ends, ((0, 0), (0, 13), (0, 0)))], axis=1)
    steps = [(s, s - 1 if s % 2 == 0 else s + 1) for s in range(1, seq_count - 1)]
    beyond = lax.ppermute(outer, SEQ, steps)

    ids_got = got[:, 3 * tok, :tok].reshape(-1)
    id_block = jnp.pad(ids_got.reshape(-1, HEAD_DIM), ((0, 16 - plane_tok // HEAD_DIM), (0, 0)))
    key_vals = jnp.concatenate(
        [got[:, tok : 3 * tok, :].reshape(2 * plane_tok, HEAD_DIM), id_block], axis=0
    )

    cells, beyond = cells.reshape(-1, lanes), beyond.reshape(-1, lanes)
    across = ring(key_vals, "xh", 1)
    across, *weights = lax.optimization_barrier((across,) + weights)
    mine = jnp.concatenate([key_vals, across, cells, beyond])
    theirs = ring(mine, "core", 1)
    sizes = key_vals.shape[0], cells.shape[0], beyond.shape[0]
    chip_cells = cores * tile_rows * tile_cols
    place = jnp.concatenate([jnp.stack([me_core, me_grp]), taps]).astype(jnp.int32)
    head_out = pl.pallas_call(
        functools.partial(attention_kernel, tok, sizes[0]),
        out_shape=jax.ShapeDtypeStruct((plane_tok, HEAD_DIM), BF),
        in_specs=[VMEM] * 4,
        out_specs=VMEM,
        compiler_params=pltpu.CompilerParams(vmem_limit_bytes=40 << 20),
        cost_estimate=pl.CostEstimate(
            flops=4 * plane_tok * plane_tok * planes * HEAD_DIM,
            bytes_accessed=planes * plane_tok * HEAD_DIM * 4,
            transcendentals=plane_tok * plane_tok * planes,
        ),
        name="attention",
    )(got, mine, theirs, ids_got.astype(F32)[:, None])
    place, head_out = lax.optimization_barrier((place, head_out))
    partial = pl.pallas_call(
        functools.partial(conv_kernel, share, sizes),
        out_shape=jax.ShapeDtypeStruct((parts, chip_cells + chip_cells // 2, 128), BF),
        in_specs=[pl.BlockSpec(memory_space=pltpu.SMEM)] + [VMEM] * (2 + len(weights)),
        out_specs=VMEM,
        scratch_shapes=[
            pltpu.VMEM((3, parts, 3, cores * tile_rows + 2, tile_cols, lanes), BF),
            pltpu.VMEM((SLOTS, lanes, 256), BF),
            pltpu.VMEM((parts, chip_cells, 256), F32),
            pltpu.VMEM((parts, chip_cells, 256), F32),
        ],
        compiler_params=pltpu.CompilerParams(vmem_limit_bytes=48 << 20),
        cost_estimate=pl.CostEstimate(
            flops=2 * parts * chip_cells * 32 * lanes * 256,
            bytes_accessed=27 * lanes * CH,
            transcendentals=0,
        ),
        name="convolution",
    )(place, mine, theirs, *weights)
    returned = exchange(head_out.reshape(heads, tok, HEAD_DIM), HEAD_AXES)

    sums_back = partial[0].astype(F32)
    for by in range(1, parts):
        sums_back = sums_back + ring(partial[by], "rep", parts - by).astype(F32)
    tile_cells = tile_rows * tile_cols
    main_cols = sums_back[:chip_cells].reshape(cores, tile_cells, 128)
    last_cols = sums_back[chip_cells:].reshape(tile_cells, cores, 64).transpose(1, 0, 2)
    both = jnp.concatenate([main_cols, last_cols], axis=2)
    keep = jnp.where(is_upper, both[0], both[1])
    give = jnp.where(is_upper, both[1], both[0]).astype(BF)
    take = ring(give, "core", 1).astype(F32)
    convolved = jnp.where(
        is_upper,
        jnp.concatenate([keep, take], axis=1),
        jnp.concatenate([take, keep], axis=1),
    ).reshape(features.shape)
    attended = returned.transpose(1, 0, 2).reshape(tok, local_cols)
    decoded = (feat_f + convolved).astype(BF)
    return (attended, decoded)


def solution(mesh):
    grid = Mesh(
        mesh.devices.reshape((2, 2, 8, 2) + mesh.devices.shape[1:]),
        ("xh", "xl", "z", "core", "grp", "rep"),
    )
    tokens = P(("rep",) + SEQ, "grp")
    image = P("rep", SEQ, "grp", None)
    placed = (
        tokens,
        tokens,
        tokens,
        P("grp"),
        P("grp"),
        P(("rep",) + SEQ),
        image,
        image,
        P(),
        P(SEQ, None),
    )
    return jax.shard_map(
        shards, mesh=grid, in_specs=placed, out_specs=(tokens, image), check_vma=False
    )
```

```python
import functools
import math

import jax
import jax.numpy as jnp
from jax import lax
from jax.experimental import pallas as pl
from jax.experimental.pallas import tpu as pltpu
from jax.sharding import Mesh
from jax.sharding import PartitionSpec as P

HEADS = 32
HEAD_DIM = 128
CH = 384
WIDTH = HEADS * HEAD_DIM
EPS = 1e-06
X = ("xh", "xl")
SEQ = ("xh", "xl", "z", "core")
HEAD_AXES = ("xl", "z")
BF = jnp.bfloat16
F32 = jnp.float32
VMEM = pl.BlockSpec(memory_space=pltpu.VMEM)


def attend(tok, q_ref, blocks, qid_ref, out_ref):
    groups = q_ref.shape[0]
    count = groups * tok
    scale = 1.0 / math.sqrt(HEAD_DIM)
    q = q_ref[:, :tok, :].reshape(count, HEAD_DIM)
    keys, vals, ids = [], [], []
    for ref in blocks:
        pairs = ref[: 2 * count, :].reshape(groups, 2 * tok, HEAD_DIM)
        keys.append(pairs[:, :tok].reshape(count, HEAD_DIM))
        vals.append(pairs[:, tok:].reshape(count, HEAD_DIM))
        rows = ref[2 * count : 2 * count + 16, :].astype(F32)
        ids.append(jnp.concatenate([rows[i : i + 1] for i in range(count // HEAD_DIM)], axis=1))
    step = 128
    for lo in range(0, count, step):
        q_id = qid_ref[lo : lo + step, :]
        scores = []
        for key, key_id in zip(keys, ids):
            s = lax.dot_general(
                q[lo : lo + step], key, (((1,), (1,)), ((), ())), preferred_element_type=F32
            )
            scores.append(jnp.where(q_id == key_id, s * scale, -1e30))
        top = functools.reduce(
            jnp.maximum, [jnp.max(s, axis=-1, keepdims=True) for s in scores]
        )
        total = jnp.zeros((step, 1), F32)
        mixed = jnp.zeros((step, HEAD_DIM), F32)
        for s, val in zip(scores, vals):
            probs = jnp.exp(s - top)
            total = total + jnp.sum(probs, axis=-1, keepdims=True)
            mixed = mixed + jnp.dot(probs.astype(BF), val, preferred_element_type=F32)
        out_ref[lo : lo + step, :] = (mixed / total).astype(BF)


def lay_out(core, left, cells_ref, halo_ref, slab_ref):
    _, parts, frames, _, cols, lanes = slab_ref.shape
    at = lax.broadcasted_iota(jnp.int32, (cols, lanes), 0)

    def put(part, t, row, cells, beside):
        wide = cells.astype(F32)
        before = jnp.where(at == 0, beside * left, pltpu.roll(wide, 1, axis=0))
        after = jnp.where(at == cols - 1, beside * (1.0 - left), pltpu.roll(wide, cols - 1, axis=0))
        slab_ref[0, part, t, row] = before.astype(BF)
        slab_ref[1, part, t, row] = cells
        slab_ref[2, part, t, row] = after.astype(BF)

    def one_part(part, _):
        base = pl.multiple_of(part * (2 * frames * cols + 16), 16)
        beside = cells_ref[pl.ds(base + 2 * frames * cols, 16), :].astype(F32)
        halo_base = pl.multiple_of(part * (frames * cols + 16), 16)
        beyond = halo_ref[pl.ds(halo_base + frames * cols, 16), :].astype(F32)
        for t in range(frames):
            for r in range(2):
                k = 2 * t + r
                cells = cells_ref[pl.ds(base + k * cols, cols), :]
                put(part, t, 1 + 2 * core + r, cells, beside[k : k + 1])
            put(part, t, 5 * core, halo_ref[pl.ds(halo_base + t * cols, cols), :], beyond[t : t + 1])
        return 0

    lax.fori_loop(0, parts, one_part, 0)


SLOTS = 8


def convolve(share, taps, order, slab_ref, planes, out_ref, pad_ref, low_ref, high_ref):
    _, parts, _, high, cols, lanes = slab_ref.shape
    rows = high - 2
    cells = rows * cols
    half = SLOTS // 2
    pad_ref[...] = jnp.zeros_like(pad_ref)
    for p, ref in enumerate(planes):
        for j in range(SLOTS):
            pad_ref[j, :share, :128] = ref[j * share : (j + 1) * share, :]
            start = SLOTS * share + (j % half) * share
            pad_ref[j, :share, 128:] = ref[start : start + share, :]
        for part in range(parts):
            for side, total_ref in ((0, low_ref), (1, high_ref)):
                pieces = []
                for j in range(half):
                    tap = jnp.minimum(taps(p) + side * half + j, 26)
                    t, r, c = tap // 9, (tap // 3) % 3, tap % 3
                    pieces.append(
                        slab_ref[c, part, t, pl.ds(r, rows), :, :].reshape(cells, lanes)
                    )
                patches = jnp.concatenate(pieces, axis=1)
                weight = pad_ref[side * half : (side + 1) * half].reshape(half * lanes, 256)
                product = jnp.dot(patches, weight, preferred_element_type=F32)
                if p == 0:
                    total_ref[part] = product
                else:
                    total_ref[part] += product
    lane = lax.broadcasted_iota(jnp.int32, (cells // 2, 128), 1)
    for part in range(parts):
        low, top = low_ref[part], high_ref[part]
        out_ref[order(part), :cells, :] = (low[:, :128] + top[:, :128]).astype(BF)
        rest = low[:, 128:] + pltpu.roll(top[:, 128:], 64, axis=1)
        rest = jnp.where(lane < 64, rest[: cells // 2], pltpu.roll(rest[cells // 2 :], 64, axis=1))
        out_ref[order(part), cells:, :] = rest.astype(BF)


def attention_kernel(tok, block, q_ref, mine_ref, theirs_ref, qid_ref, out_ref):
    blocks = [r.at[pl.ds(i * block, block)] for r in (mine_ref, theirs_ref) for i in range(2)]
    attend(tok, q_ref, blocks, qid_ref, out_ref)


def conv_kernel(share, sizes, place_ref, mine_ref, theirs_ref, *refs):
    *planes, conv_ref, slab_ref, pad_ref, low_ref, high_ref = refs
    block, cells, halo = sizes
    core, left = place_ref[0], place_ref[1].astype(F32)
    for own, ref in ((core, mine_ref), (1 - core, theirs_ref)):
        lay_out(
            own, left, ref.at[pl.ds(2 * block, cells)], ref.at[pl.ds(2 * block + cells, halo)], slab_ref
        )
    convolve(
        share, lambda p: place_ref[2 + p], lambda i: place_ref[2 + len(planes) + i],
        slab_ref, planes, conv_ref, pad_ref, low_ref, high_ref,
    )


def activate(cells, gain):
    cells = cells.astype(F32)
    scale = lax.rsqrt(jnp.mean(cells * cells, axis=-1, keepdims=True) + EPS)
    return jax.nn.silu(cells * scale * gain).astype(BF)


def three_parts(total):
    high = lax.reduce_precision(total, 8, 7)
    mid = lax.reduce_precision(total - high, 8, 7)
    return jnp.stack([high, mid, (total - high) - mid]).astype(BF)


def ring(data, axis, by):
    count = lax.axis_size(axis)
    return lax.ppermute(data, axis, [(i, (i + by) % count) for i in range(count)])


def swap(data, axis, bit):
    return lax.ppermute(data, axis, [(i, i ^ bit) for i in range(lax.axis_size(axis))])


def planes_of(data):
    count = lax.axis_size(X)
    return ring(data, X, 1), ring(data, X, count - 1), ring(data, X, 2)


def exchange(data, axes):
    return lax.all_to_all(data, axes, split_axis=0, concat_axis=0, tiled=True)


def shards(
    queries, keys, values, q_gain, k_gain, clip_ids, features, frame_cache, feat_gain, conv_weight
):
    tok, local_cols = queries.shape
    heads = local_cols // HEAD_DIM
    planes = lax.axis_size(X)
    plane_tok = heads * tok
    deep, cores = lax.axis_size("z"), lax.axis_size("core")
    seq_count = planes * deep * cores
    me_x, me_core = lax.axis_index(X), lax.axis_index("core")
    me_grp, me_rep = lax.axis_index("grp"), lax.axis_index("rep")
    parts = lax.axis_size("rep")
    order = jnp.stack([me_x, me_x - 1, me_x + 1, me_x + 2]) % planes

    q_f, k_f = queries.astype(F32), keys.astype(F32)
    sums = jnp.stack([jnp.sum(q_f * q_f, axis=-1), jnp.sum(k_f * k_f, axis=-1)])
    lanes = 128
    frames, tile_rows, tile_cols, _ = features.shape
    is_left, is_upper = me_grp == 0, me_core == 0
    raw_edge = jnp.concatenate(
        [
            jnp.where(is_left, frame_cache[:, :, -1], frame_cache[:, :, 0]),
            jnp.where(is_left, features[:, :, -1], features[:, :, 0]),
        ]
    )
    edge_count = raw_edge.shape[0] * raw_edge.shape[1]
    first_out = jnp.concatenate(
        [
            jnp.pad(three_parts(sums).reshape(6, tok), ((0, 0), (0, lanes - tok))),
            raw_edge.reshape(-1, lanes),
        ]
    )
    first_in = ring(first_out, "grp", 1)
    theirs = first_in[:6, :tok].astype(F32).reshape(3, 2, tok)
    sums = sums + ((theirs[0] + theirs[1]) + theirs[2])
    beside = first_in[6:].reshape(edge_count, CH)

    share = CH // parts
    weight_rows = conv_weight.shape[0]
    first = (me_rep + 2 * me_core) % parts
    held = jnp.arange(48)[:, None]
    late = (me_core == 1) & (me_rep >= 2)
    source = jnp.where(
        held < 40,
        4 * (held + late.astype(jnp.int32)) + first,
        jnp.where((held == 40) & (first < 2), jnp.where(me_core == 1, first, 160 + first), -1),
    )
    pick = (source == jnp.arange(weight_rows)[None, :]).astype(BF)
    chosen = jnp.dot(pick, conv_weight, preferred_element_type=F32).astype(BF)
    halves = chosen.reshape(48, cores, CH // cores).transpose(1, 0, 2)
    last = halves[:, :, 128:]
    halves = jnp.concatenate(
        [halves[:, :, :128], jnp.concatenate([last[:, :24], last[:, 24:]], axis=2)], axis=1
    )
    sent_weight = jnp.broadcast_to(halves[None], (deep,) + halves.shape).reshape(-1, 72, 128)
    plane_weight = exchange(sent_weight, ("z", "core"))

    scales = lax.rsqrt(sums / WIDTH + EPS)
    q_norm = (q_f * scales[0][:, None] * q_gain).astype(BF)
    k_norm = (k_f * scales[1][:, None] * k_gain).astype(BF)
    id_row = jnp.pad(clip_ids.astype(BF)[None, :], ((0, 7), (0, HEAD_DIM - tok)))

    def by_head(data):
        return data.reshape(tok, heads, HEAD_DIM).transpose(1, 0, 2)

    payload = jnp.concatenate(
        [
            by_head(q_norm),
            by_head(k_norm),
            by_head(values),
            jnp.broadcast_to(id_row[None], (heads,) + id_row.shape),
        ],
        axis=1,
    )
    got = exchange(payload, HEAD_AXES)
    slot = jnp.arange(deep * cores * 48)
    spot, item = slot // 48, slot % 48
    target = 81 * (spot // cores) + jnp.where(item == 40, 40, item + 41 * (spot % cores))
    target = jnp.where(item > 40, -1, target + (648 * me_x) % share)
    place = (jnp.arange(SLOTS * share)[:, None] == target[None, :]).astype(BF)
    place = place.reshape(SLOTS * share, deep * cores, 48)
    main = plane_weight[:, :48, :]
    rest = plane_weight[:, 48:, :]

    def placed_rows(at, data):
        return lax.dot_general(
            at, data, (((1, 2), (0, 1)), ((), ())), preferred_element_type=F32
        ).astype(BF)

    last_cols = (
        placed_rows(place[:, :, :24], rest)[:, :64] + placed_rows(place[:, :, 24:], rest)[:, 64:]
    )
    split = SLOTS * share // 2
    my_weight = jnp.concatenate(
        [
            placed_rows(place, main),
            jnp.concatenate([last_cols[:split], last_cols[split:]], axis=1),
        ],
        axis=0,
    )
    weights = (my_weight,) + planes_of(my_weight)
    taps = (27 * order) // planes
    got, before = lax.optimization_barrier((got, weights[1]))
    weights = (weights[0], before) + weights[2:]

    feat_f = features.astype(F32)
    stacked = jnp.concatenate([frame_cache, activate(features, feat_gain)], axis=0)
    lane = jnp.arange(parts * lanes)
    chan = jnp.where(
        lane % lanes < share, parts * (lane % lanes) + (me_rep + lane // lanes) % parts, -1
    )
    sort = (jnp.arange(CH)[:, None] == chan[None, :]).astype(BF)

    def by_class(data):
        data = jnp.dot(data, sort, preferred_element_type=F32).astype(BF)
        return data.reshape(-1, parts, lanes).transpose(1, 0, 2)

    beside = jnp.concatenate([beside[:-2], activate(beside[-2:], feat_gain)])
    beside = jnp.pad(beside, ((0, 16 - edge_count), (0, 0)))
    outgoing = jnp.concatenate([by_class(stacked.reshape(-1, CH)), by_class(beside)], axis=1)
    cells = jnp.stack([outgoing[0]] + [ring(outgoing[by], "rep", by) for by in range(1, parts)])
    main = cells[:, : 6 * tile_cols].reshape(parts, 3, tile_rows, tile_cols, lanes)
    ends = cells[:, 6 * tile_cols : 6 * tile_cols + 6].reshape(parts, 3, tile_rows, lanes)
    outer = jnp.where(is_upper, main[:, :, 0], main[:, :, -1]).reshape(parts, -1, lanes)
    outer_ends = jnp.where(is_upper, ends[:, :, 0], ends[:, :, -1])
    outer = jnp.concatenate([outer, jnp.pad(outer_ends, ((0, 0), (0, 13), (0, 0)))], axis=1)
    steps = [(s, s - 1 if s % 2 == 0 else s + 1) for s in range(1, seq_count - 1)]
    beyond = lax.ppermute(outer, SEQ, steps)

    ids_got = got[:, 3 * tok, :tok].reshape(-1)
    id_block = jnp.pad(ids_got.reshape(-1, HEAD_DIM), ((0, 16 - plane_tok // HEAD_DIM), (0, 0)))
    key_vals = jnp.concatenate(
        [got[:, tok : 3 * tok, :].reshape(2 * plane_tok, HEAD_DIM), id_block], axis=0
    )

    cells, beyond = cells.reshape(-1, lanes), beyond.reshape(-1, lanes)
    across = ring(key_vals, "xh", 1)
    across, *weights = lax.optimization_barrier((across,) + weights)
    mine = jnp.concatenate([key_vals, across, cells, beyond])
    theirs = ring(mine, "core", 1)
    sizes = key_vals.shape[0], cells.shape[0], beyond.shape[0]
    chip_cells = cores * tile_rows * tile_cols
    spots = me_rep ^ ((me_rep - jnp.arange(parts)) % parts)
    place = jnp.concatenate([jnp.stack([me_core, me_grp]), taps, spots]).astype(jnp.int32)
    head_out = pl.pallas_call(
        functools.partial(attention_kernel, tok, sizes[0]),
        out_shape=jax.ShapeDtypeStruct((plane_tok, HEAD_DIM), BF),
        in_specs=[VMEM] * 4,
        out_specs=VMEM,
        compiler_params=pltpu.CompilerParams(vmem_limit_bytes=40 << 20),
        cost_estimate=pl.CostEstimate(
            flops=4 * plane_tok * plane_tok * planes * HEAD_DIM,
            bytes_accessed=planes * plane_tok * HEAD_DIM * 4,
            transcendentals=plane_tok * plane_tok * planes,
        ),
        name="attention",
    )(got, mine, theirs, ids_got.astype(F32)[:, None])
    place, head_out = lax.optimization_barrier((place, head_out))
    partial = pl.pallas_call(
        functools.partial(conv_kernel, share, sizes),
        out_shape=jax.ShapeDtypeStruct((parts, chip_cells + chip_cells // 2, 128), BF),
        in_specs=[pl.BlockSpec(memory_space=pltpu.SMEM)] + [VMEM] * (2 + len(weights)),
        out_specs=VMEM,
        scratch_shapes=[
            pltpu.VMEM((3, parts, 3, cores * tile_rows + 2, tile_cols, lanes), BF),
            pltpu.VMEM((SLOTS, lanes, 256), BF),
            pltpu.VMEM((parts, chip_cells, 256), F32),
            pltpu.VMEM((parts, chip_cells, 256), F32),
        ],
        compiler_params=pltpu.CompilerParams(vmem_limit_bytes=48 << 20),
        cost_estimate=pl.CostEstimate(
            flops=2 * parts * chip_cells * 32 * lanes * 256,
            bytes_accessed=27 * lanes * CH,
            transcendentals=0,
        ),
        name="convolution",
    )(place, mine, theirs, *weights)
    returned = exchange(head_out.reshape(heads, tok, HEAD_DIM), HEAD_AXES)

    from_two = swap(partial[2:], "rep", 2)
    sums_back = partial[:2].astype(F32) + from_two.astype(F32)
    sums_back = sums_back[0] + swap(sums_back[1].astype(BF), "rep", 1).astype(F32)
    tile_cells = tile_rows * tile_cols
    main_cols = sums_back[:chip_cells].reshape(cores, tile_cells, 128)
    last_cols = sums_back[chip_cells:].reshape(tile_cells, cores, 64).transpose(1, 0, 2)
    both = jnp.concatenate([main_cols, last_cols], axis=2)
    keep = jnp.where(is_upper, both[0], both[1])
    give = jnp.where(is_upper, both[1], both[0]).astype(BF)
    take = ring(give, "core", 1).astype(F32)
    convolved = jnp.where(
        is_upper,
        jnp.concatenate([keep, take], axis=1),
        jnp.concatenate([take, keep], axis=1),
    ).reshape(features.shape)
    attended = returned.transpose(1, 0, 2).reshape(tok, local_cols)
    decoded = (feat_f + convolved).astype(BF)
    return (attended, decoded)


def solution(mesh):
    grid = Mesh(
        mesh.devices.reshape((2, 2, 8, 2) + mesh.devices.shape[1:]),
        ("xh", "xl", "z", "core", "grp", "rep"),
    )
    tokens = P(("rep",) + SEQ, "grp")
    image = P("rep", SEQ, "grp", None)
    placed = (
        tokens,
        tokens,
        tokens,
        P("grp"),
        P("grp"),
        P(("rep",) + SEQ),
        image,
        image,
        P(),
        P(SEQ, None),
    )
    return jax.shard_map(
        shards, mesh=grid, in_specs=placed, out_specs=(tokens, image), check_vma=False
    )
```

```python
import functools
import math

import jax
import jax.numpy as jnp
from jax import lax
from jax.experimental import pallas as pl
from jax.experimental.pallas import tpu as pltpu
from jax.sharding import Mesh
from jax.sharding import PartitionSpec as P

HEADS = 32
HEAD_DIM = 128
CH = 384
WIDTH = HEADS * HEAD_DIM
EPS = 1e-06
X = ("xh", "xl")
SEQ = ("xh", "xl", "z", "core")
HEAD_AXES = ("xl", "z")
BF = jnp.bfloat16
F32 = jnp.float32
VMEM = pl.BlockSpec(memory_space=pltpu.VMEM)


def attend(tok, q_ref, blocks, qid_ref, out_ref):
    groups = q_ref.shape[0]
    count = groups * tok
    scale = 1.0 / math.sqrt(HEAD_DIM)
    q = q_ref[:, :tok, :].reshape(count, HEAD_DIM)
    keys, vals, ids = [], [], []
    for ref in blocks:
        pairs = ref[: 2 * count, :].reshape(groups, 2 * tok, HEAD_DIM)
        keys.append(pairs[:, :tok].reshape(count, HEAD_DIM))
        vals.append(pairs[:, tok:].reshape(count, HEAD_DIM))
        rows = ref[2 * count : 2 * count + 16, :].astype(F32)
        ids.append(jnp.concatenate([rows[i : i + 1] for i in range(count // HEAD_DIM)], axis=1))
    step = 128
    for lo in range(0, count, step):
        q_id = qid_ref[lo : lo + step, :]
        scores = []
        for key, key_id in zip(keys, ids):
            s = lax.dot_general(
                q[lo : lo + step], key, (((1,), (1,)), ((), ())), preferred_element_type=F32
            )
            scores.append(jnp.where(q_id == key_id, s * scale, -1e30))
        top = functools.reduce(
            jnp.maximum, [jnp.max(s, axis=-1, keepdims=True) for s in scores]
        )
        total = jnp.zeros((step, 1), F32)
        mixed = jnp.zeros((step, HEAD_DIM), F32)
        for s, val in zip(scores, vals):
            probs = jnp.exp(s - top)
            total = total + jnp.sum(probs, axis=-1, keepdims=True)
            mixed = mixed + jnp.dot(probs.astype(BF), val, preferred_element_type=F32)
        out_ref[lo : lo + step, :] = (mixed / total).astype(BF)


def lay_out(core, left, cells_ref, halo_ref, slab_ref):
    _, parts, frames, _, cols, lanes = slab_ref.shape
    at = lax.broadcasted_iota(jnp.int32, (cols, lanes), 0)

    def put(part, t, row, cells, beside):
        wide = cells.astype(F32)
        before = jnp.where(at == 0, beside * left, pltpu.roll(wide, 1, axis=0))
        after = jnp.where(at == cols - 1, beside * (1.0 - left), pltpu.roll(wide, cols - 1, axis=0))
        slab_ref[0, part, t, row] = before.astype(BF)
        slab_ref[1, part, t, row] = cells
        slab_ref[2, part, t, row] = after.astype(BF)

    def one_part(part, _):
        base = pl.multiple_of(part * (2 * frames * cols + 16), 16)
        beside = cells_ref[pl.ds(base + 2 * frames * cols, 16), :].astype(F32)
        halo_base = pl.multiple_of(part * (frames * cols + 16), 16)
        beyond = halo_ref[pl.ds(halo_base + frames * cols, 16), :].astype(F32)
        for t in range(frames):
            for r in range(2):
                k = 2 * t + r
                cells = cells_ref[pl.ds(base + k * cols, cols), :]
                put(part, t, 1 + 2 * core + r, cells, beside[k : k + 1])
            put(part, t, 5 * core, halo_ref[pl.ds(halo_base + t * cols, cols), :], beyond[t : t + 1])
        return 0

    lax.fori_loop(0, parts, one_part, 0)


SLOTS = 8


def convolve(share, taps, order, slab_ref, planes, out_ref, pad_ref, low_ref, high_ref):
    _, parts, _, high, cols, lanes = slab_ref.shape
    rows = high - 2
    cells = rows * cols
    half = SLOTS // 2
    pad_ref[...] = jnp.zeros_like(pad_ref)
    for p, ref in enumerate(planes):
        for j in range(SLOTS):
            pad_ref[j, :share, :128] = ref[j * share : (j + 1) * share, :]
            start = SLOTS * share + (j % half) * share
            pad_ref[j, :share, 128:] = ref[start : start + share, :]
        for part in range(parts):
            for side, total_ref in ((0, low_ref), (1, high_ref)):
                pieces = []
                for j in range(half):
                    tap = jnp.minimum(taps(p) + side * half + j, 26)
                    t, r, c = tap // 9, (tap // 3) % 3, tap % 3
                    pieces.append(
                        slab_ref[c, part, t, pl.ds(r, rows), :, :].reshape(cells, lanes)
                    )
                patches = jnp.concatenate(pieces, axis=1)
                weight = pad_ref[side * half : (side + 1) * half].reshape(half * lanes, 256)
                product = jnp.dot(patches, weight, preferred_element_type=F32)
                if p == 0:
                    total_ref[part] = product
                else:
                    total_ref[part] += product
    lane = lax.broadcasted_iota(jnp.int32, (cells // 2, 128), 1)
    for part in range(parts):
        low, top = low_ref[part], high_ref[part]
        out_ref[order(part), :cells, :] = (low[:, :128] + top[:, :128]).astype(BF)
        rest = low[:, 128:] + pltpu.roll(top[:, 128:], 64, axis=1)
        rest = jnp.where(lane < 64, rest[: cells // 2], pltpu.roll(rest[cells // 2 :], 64, axis=1))
        out_ref[order(part), cells:, :] = rest.astype(BF)


def attention_kernel(tok, block, q_ref, mine_ref, theirs_ref, qid_ref, out_ref):
    blocks = [r.at[pl.ds(i * block, block)] for r in (mine_ref, theirs_ref) for i in range(2)]
    attend(tok, q_ref, blocks, qid_ref, out_ref)


def conv_kernel(share, sizes, place_ref, mine_ref, theirs_ref, *refs):
    *planes, conv_ref, slab_ref, pad_ref, low_ref, high_ref = refs
    block, cells, halo = sizes
    core, left = place_ref[0], place_ref[1].astype(F32)
    for own, ref in ((core, mine_ref), (1 - core, theirs_ref)):
        lay_out(
            own, left, ref.at[pl.ds(2 * block, cells)], ref.at[pl.ds(2 * block + cells, halo)], slab_ref
        )
    convolve(
        share, lambda p: place_ref[2 + p], lambda i: place_ref[2 + len(planes) + i],
        slab_ref, planes, conv_ref, pad_ref, low_ref, high_ref,
    )


def activate(cells, gain):
    cells = cells.astype(F32)
    scale = lax.rsqrt(jnp.mean(cells * cells, axis=-1, keepdims=True) + EPS)
    return jax.nn.silu(cells * scale * gain).astype(BF)


def three_parts(total):
    high = lax.reduce_precision(total, 8, 7)
    mid = lax.reduce_precision(total - high, 8, 7)
    return jnp.stack([high, mid, (total - high) - mid]).astype(BF)


def ring(data, axis, by):
    count = lax.axis_size(axis)
    return lax.ppermute(data, axis, [(i, (i + by) % count) for i in range(count)])


def swap(data, axis, bit):
    return lax.ppermute(data, axis, [(i, i ^ bit) for i in range(lax.axis_size(axis))])


def planes_of(data):
    count = lax.axis_size(X)
    return ring(data, X, 1), ring(data, X, count - 1), ring(data, X, 2)


def exchange(data, axes):
    return lax.all_to_all(data, axes, split_axis=0, concat_axis=0, tiled=True)


def shards(
    queries, keys, values, q_gain, k_gain, clip_ids, features, frame_cache, feat_gain, conv_weight
):
    tok, local_cols = queries.shape
    heads = local_cols // HEAD_DIM
    planes = lax.axis_size(X)
    plane_tok = heads * tok
    deep, cores = lax.axis_size("z"), lax.axis_size("core")
    seq_count = planes * deep * cores
    me_x, me_core = lax.axis_index(X), lax.axis_index("core")
    me_grp, me_rep = lax.axis_index("grp"), lax.axis_index("rep")
    parts = lax.axis_size("rep")
    order = jnp.stack([me_x, me_x - 1, me_x + 1, me_x + 2]) % planes

    q_f, k_f = queries.astype(F32), keys.astype(F32)
    sums = jnp.stack([jnp.sum(q_f * q_f, axis=-1), jnp.sum(k_f * k_f, axis=-1)])
    lanes = 128
    frames, tile_rows, tile_cols, _ = features.shape
    is_left, is_upper = me_grp == 0, me_core == 0
    raw_edge = jnp.concatenate(
        [
            jnp.where(is_left, frame_cache[:, :, -1], frame_cache[:, :, 0]),
            jnp.where(is_left, features[:, :, -1], features[:, :, 0]),
        ]
    )
    edge_count = raw_edge.shape[0] * raw_edge.shape[1]
    first_out = jnp.concatenate(
        [
            jnp.pad(three_parts(sums).reshape(6, tok), ((0, 0), (0, lanes - tok))),
            raw_edge.reshape(-1, lanes),
        ]
    )
    first_in = ring(first_out, "grp", 1)
    theirs = first_in[:6, :tok].astype(F32).reshape(3, 2, tok)
    sums = sums + ((theirs[0] + theirs[1]) + theirs[2])
    beside = first_in[6:].reshape(edge_count, CH)

    share = CH // parts
    weight_rows = conv_weight.shape[0]
    first = (me_rep + 2 * me_core) % parts
    held = jnp.arange(48)[:, None]
    late = (me_core == 1) & (me_rep >= 2)
    source = jnp.where(
        held < 40,
        4 * (held + late.astype(jnp.int32)) + first,
        jnp.where((held == 40) & (first < 2), jnp.where(me_core == 1, first, 160 + first), -1),
    )
    pick = (source == jnp.arange(weight_rows)[None, :]).astype(BF)
    chosen = jnp.dot(pick, conv_weight, preferred_element_type=F32).astype(BF)
    halves = chosen.reshape(48, cores, CH // cores).transpose(1, 0, 2)
    last = halves[:, :, 128:]
    halves = jnp.concatenate(
        [halves[:, :, :128], jnp.concatenate([last[:, :24], last[:, 24:]], axis=2)], axis=1
    )
    sent_weight = jnp.broadcast_to(halves[None], (deep,) + halves.shape).reshape(-1, 72, 128)
    plane_weight = exchange(sent_weight, ("z", "core"))

    scales = lax.rsqrt(sums / WIDTH + EPS)
    q_norm = (q_f * scales[0][:, None] * q_gain).astype(BF)
    k_norm = (k_f * scales[1][:, None] * k_gain).astype(BF)
    id_row = jnp.pad(clip_ids.astype(BF)[None, :], ((0, 7), (0, HEAD_DIM - tok)))

    def by_head(data):
        return data.reshape(tok, heads, HEAD_DIM).transpose(1, 0, 2)

    payload = jnp.concatenate(
        [
            by_head(q_norm),
            by_head(k_norm),
            by_head(values),
            jnp.broadcast_to(id_row[None], (heads,) + id_row.shape),
        ],
        axis=1,
    )
    got = exchange(payload, HEAD_AXES)
    slot = jnp.arange(deep * cores * 48)
    spot, item = slot // 48, slot % 48
    target = 81 * (spot // cores) + jnp.where(item == 40, 40, item + 41 * (spot % cores))
    target = jnp.where(item > 40, -1, target + (648 * me_x) % share)
    place = (jnp.arange(SLOTS * share)[:, None] == target[None, :]).astype(BF)
    place = place.reshape(SLOTS * share, deep * cores, 48)
    main = plane_weight[:, :48, :]
    rest = plane_weight[:, 48:, :]

    def placed_rows(at, data):
        return lax.dot_general(
            at, data, (((1, 2), (0, 1)), ((), ())), preferred_element_type=F32
        ).astype(BF)

    last_cols = (
        placed_rows(place[:, :, :24], rest)[:, :64] + placed_rows(place[:, :, 24:], rest)[:, 64:]
    )
    split = SLOTS * share // 2
    my_weight = jnp.concatenate(
        [
            placed_rows(place, main),
            jnp.concatenate([last_cols[:split], last_cols[split:]], axis=1),
        ],
        axis=0,
    )
    weights = (my_weight,) + planes_of(my_weight)
    taps = (27 * order) // planes
    got, before = lax.optimization_barrier((got, weights[1]))
    weights = (weights[0], before) + weights[2:]

    feat_f = features.astype(F32)
    stacked = jnp.concatenate([frame_cache, activate(features, feat_gain)], axis=0)
    lane = jnp.arange(parts * lanes)
    slot = lane // lanes
    kind = me_rep ^ (2 * (slot % 2) + slot // 2)
    chan = jnp.where(lane % lanes < share, parts * (lane % lanes) + kind, -1)
    sort = (jnp.arange(CH)[:, None] == chan[None, :]).astype(BF)

    def by_class(data):
        data = jnp.dot(data, sort, preferred_element_type=F32).astype(BF)
        return data.reshape(-1, parts, lanes).transpose(1, 0, 2)

    beside = jnp.concatenate([beside[:-2], activate(beside[-2:], feat_gain)])
    beside = jnp.pad(beside, ((0, 16 - edge_count), (0, 0)))
    outgoing = jnp.concatenate([by_class(stacked.reshape(-1, CH)), by_class(beside)], axis=1)
    from_one = swap(outgoing[2:], "rep", 1)
    from_two = swap(jnp.stack([outgoing[1], from_one[1]]), "rep", 2)
    cells = jnp.concatenate([jnp.stack([outgoing[0], from_one[0]]), from_two])
    main = cells[:, : 6 * tile_cols].reshape(parts, 3, tile_rows, tile_cols, lanes)
    ends = cells[:, 6 * tile_cols : 6 * tile_cols + 6].reshape(parts, 3, tile_rows, lanes)
    outer = jnp.where(is_upper, main[:, :, 0], main[:, :, -1]).reshape(parts, -1, lanes)
    outer_ends = jnp.where(is_upper, ends[:, :, 0], ends[:, :, -1])
    outer = jnp.concatenate([outer, jnp.pad(outer_ends, ((0, 0), (0, 13), (0, 0)))], axis=1)
    steps = [(s, s - 1 if s % 2 == 0 else s + 1) for s in range(1, seq_count - 1)]
    beyond = lax.ppermute(outer, SEQ, steps)

    ids_got = got[:, 3 * tok, :tok].reshape(-1)
    id_block = jnp.pad(ids_got.reshape(-1, HEAD_DIM), ((0, 16 - plane_tok // HEAD_DIM), (0, 0)))
    key_vals = jnp.concatenate(
        [got[:, tok : 3 * tok, :].reshape(2 * plane_tok, HEAD_DIM), id_block], axis=0
    )

    cells, beyond = cells.reshape(-1, lanes), beyond.reshape(-1, lanes)
    across = ring(key_vals, "xh", 1)
    across, *weights = lax.optimization_barrier((across,) + weights)
    mine = jnp.concatenate([key_vals, across, cells, beyond])
    theirs = ring(mine, "core", 1)
    sizes = key_vals.shape[0], cells.shape[0], beyond.shape[0]
    chip_cells = cores * tile_rows * tile_cols
    spots = jnp.arange(parts)
    place = jnp.concatenate([jnp.stack([me_core, me_grp]), taps, spots]).astype(jnp.int32)
    head_out = pl.pallas_call(
        functools.partial(attention_kernel, tok, sizes[0]),
        out_shape=jax.ShapeDtypeStruct((plane_tok, HEAD_DIM), BF),
        in_specs=[VMEM] * 4,
        out_specs=VMEM,
        compiler_params=pltpu.CompilerParams(vmem_limit_bytes=40 << 20),
        cost_estimate=pl.CostEstimate(
            flops=4 * plane_tok * plane_tok * planes * HEAD_DIM,
            bytes_accessed=planes * plane_tok * HEAD_DIM * 4,
            transcendentals=plane_tok * plane_tok * planes,
        ),
        name="attention",
    )(got, mine, theirs, ids_got.astype(F32)[:, None])
    place, head_out = lax.optimization_barrier((place, head_out))
    partial = pl.pallas_call(
        functools.partial(conv_kernel, share, sizes),
        out_shape=jax.ShapeDtypeStruct((parts, chip_cells + chip_cells // 2, 128), BF),
        in_specs=[pl.BlockSpec(memory_space=pltpu.SMEM)] + [VMEM] * (2 + len(weights)),
        out_specs=VMEM,
        scratch_shapes=[
            pltpu.VMEM((3, parts, 3, cores * tile_rows + 2, tile_cols, lanes), BF),
            pltpu.VMEM((SLOTS, lanes, 256), BF),
            pltpu.VMEM((parts, chip_cells, 256), F32),
            pltpu.VMEM((parts, chip_cells, 256), F32),
        ],
        compiler_params=pltpu.CompilerParams(vmem_limit_bytes=48 << 20),
        cost_estimate=pl.CostEstimate(
            flops=2 * parts * chip_cells * 32 * lanes * 256,
            bytes_accessed=27 * lanes * CH,
            transcendentals=0,
        ),
        name="convolution",
    )(place, mine, theirs, *weights)
    returned = exchange(head_out.reshape(heads, tok, HEAD_DIM), HEAD_AXES)

    from_two = swap(partial[2:], "rep", 2)
    sums_back = partial[:2].astype(F32) + from_two.astype(F32)
    sums_back = sums_back[0] + swap(sums_back[1].astype(BF), "rep", 1).astype(F32)
    tile_cells = tile_rows * tile_cols
    main_cols = sums_back[:chip_cells].reshape(cores, tile_cells, 128)
    last_cols = sums_back[chip_cells:].reshape(tile_cells, cores, 64).transpose(1, 0, 2)
    both = jnp.concatenate([main_cols, last_cols], axis=2)
    keep = jnp.where(is_upper, both[0], both[1])
    give = jnp.where(is_upper, both[1], both[0]).astype(BF)
    take = ring(give, "core", 1).astype(F32)
    convolved = jnp.where(
        is_upper,
        jnp.concatenate([keep, take], axis=1),
        jnp.concatenate([take, keep], axis=1),
    ).reshape(features.shape)
    attended = returned.transpose(1, 0, 2).reshape(tok, local_cols)
    decoded = (feat_f + convolved).astype(BF)
    return (attended, decoded)


def solution(mesh):
    grid = Mesh(
        mesh.devices.reshape((2, 2, 8, 2) + mesh.devices.shape[1:]),
        ("xh", "xl", "z", "core", "grp", "rep"),
    )
    tokens = P(("rep",) + SEQ, "grp")
    image = P("rep", SEQ, "grp", None)
    placed = (
        tokens,
        tokens,
        tokens,
        P("grp"),
        P("grp"),
        P(("rep",) + SEQ),
        image,
        image,
        P(),
        P(SEQ, None),
    )
    return jax.shard_map(
        shards, mesh=grid, in_specs=placed, out_specs=(tokens, image), check_vma=False
    )
```

```python
import functools
import math

import jax
import jax.numpy as jnp
from jax import lax
from jax.experimental import pallas as pl
from jax.experimental.pallas import tpu as pltpu
from jax.sharding import Mesh
from jax.sharding import PartitionSpec as P

HEADS = 32
HEAD_DIM = 128
CH = 384
WIDTH = HEADS * HEAD_DIM
EPS = 1e-06
X = ("xh", "xl")
SEQ = ("xh", "xl", "z", "core")
HEAD_AXES = ("xl", "z")
BF = jnp.bfloat16
F32 = jnp.float32
VMEM = pl.BlockSpec(memory_space=pltpu.VMEM)


def attend(tok, q_ref, blocks, qid_ref, out_ref):
    groups = q_ref.shape[0]
    count = groups * tok
    scale = 1.0 / math.sqrt(HEAD_DIM)
    q = q_ref[:, :tok, :].reshape(count, HEAD_DIM)
    keys, vals, ids = [], [], []
    for ref in blocks:
        pairs = ref[: 2 * count, :].reshape(groups, 2 * tok, HEAD_DIM)
        keys.append(pairs[:, :tok].reshape(count, HEAD_DIM))
        vals.append(pairs[:, tok:].reshape(count, HEAD_DIM))
        rows = ref[2 * count : 2 * count + 16, :].astype(F32)
        ids.append(jnp.concatenate([rows[i : i + 1] for i in range(count // HEAD_DIM)], axis=1))
    step = 128
    for lo in range(0, count, step):
        q_id = qid_ref[lo : lo + step, :]
        scores = []
        for key, key_id in zip(keys, ids):
            s = lax.dot_general(
                q[lo : lo + step], key, (((1,), (1,)), ((), ())), preferred_element_type=F32
            )
            scores.append(jnp.where(q_id == key_id, s * scale, -1e30))
        top = functools.reduce(
            jnp.maximum, [jnp.max(s, axis=-1, keepdims=True) for s in scores]
        )
        total = jnp.zeros((step, 1), F32)
        mixed = jnp.zeros((step, HEAD_DIM), F32)
        for s, val in zip(scores, vals):
            probs = jnp.exp(s - top)
            total = total + jnp.sum(probs, axis=-1, keepdims=True)
            mixed = mixed + jnp.dot(probs.astype(BF), val, preferred_element_type=F32)
        out_ref[lo : lo + step, :] = (mixed / total).astype(BF)


def lay_out(core, left, cells_ref, halo_ref, slab_ref):
    _, parts, frames, _, cols, lanes = slab_ref.shape
    at = lax.broadcasted_iota(jnp.int32, (cols, lanes), 0)

    def put(part, t, row, cells, beside):
        wide = cells.astype(F32)
        before = jnp.where(at == 0, beside * left, pltpu.roll(wide, 1, axis=0))
        after = jnp.where(at == cols - 1, beside * (1.0 - left), pltpu.roll(wide, cols - 1, axis=0))
        slab_ref[0, part, t, row] = before.astype(BF)
        slab_ref[1, part, t, row] = cells
        slab_ref[2, part, t, row] = after.astype(BF)

    def one_part(part, _):
        base = pl.multiple_of(part * (2 * frames * cols + 16), 16)
        beside = cells_ref[pl.ds(base + 2 * frames * cols, 16), :].astype(F32)
        halo_base = pl.multiple_of(part * (frames * cols + 16), 16)
        beyond = halo_ref[pl.ds(halo_base + frames * cols, 16), :].astype(F32)
        for t in range(frames):
            for r in range(2):
                k = 2 * t + r
                cells = cells_ref[pl.ds(base + k * cols, cols), :]
                put(part, t, 1 + 2 * core + r, cells, beside[k : k + 1])
            put(part, t, 5 * core, halo_ref[pl.ds(halo_base + t * cols, cols), :], beyond[t : t + 1])
        return 0

    lax.fori_loop(0, parts, one_part, 0)


SLOTS = 8


def convolve(share, taps, order, slab_ref, planes, out_ref, pad_ref, low_ref, high_ref):
    _, parts, _, high, cols, lanes = slab_ref.shape
    rows = high - 2
    cells = rows * cols
    half = SLOTS // 2
    pad_ref[...] = jnp.zeros_like(pad_ref)
    for p, ref in enumerate(planes):
        for j in range(SLOTS):
            pad_ref[j, :share, :128] = ref[j * share : (j + 1) * share, :]
            start = SLOTS * share + (j % half) * share
            pad_ref[j, :share, 128:] = ref[start : start + share, :]
        for part in range(parts):
            for side, total_ref in ((0, low_ref), (1, high_ref)):
                pieces = []
                for j in range(half):
                    tap = jnp.minimum(taps(p) + side * half + j, 26)
                    t, r, c = tap // 9, (tap // 3) % 3, tap % 3
                    pieces.append(
                        slab_ref[c, part, t, pl.ds(r, rows), :, :].reshape(cells, lanes)
                    )
                patches = jnp.concatenate(pieces, axis=1)
                weight = pad_ref[side * half : (side + 1) * half].reshape(half * lanes, 256)
                product = jnp.dot(patches, weight, preferred_element_type=F32)
                if p == 0:
                    total_ref[part] = product
                else:
                    total_ref[part] += product
    lane = lax.broadcasted_iota(jnp.int32, (cells // 2, 128), 1)
    for part in range(parts):
        low, top = low_ref[part], high_ref[part]
        out_ref[order(part), :cells, :] = (low[:, :128] + top[:, :128]).astype(BF)
        rest = low[:, 128:] + pltpu.roll(top[:, 128:], 64, axis=1)
        rest = jnp.where(lane < 64, rest[: cells // 2], pltpu.roll(rest[cells // 2 :], 64, axis=1))
        out_ref[order(part), cells:, :] = rest.astype(BF)


def attention_kernel(tok, block, q_ref, mine_ref, theirs_ref, qid_ref, out_ref):
    blocks = [r.at[pl.ds(i * block, block)] for r in (mine_ref, theirs_ref) for i in range(2)]
    attend(tok, q_ref, blocks, qid_ref, out_ref)


def conv_kernel(share, sizes, place_ref, mine_ref, theirs_ref, *refs):
    *planes, conv_ref, slab_ref, pad_ref, low_ref, high_ref = refs
    block, cells, halo = sizes
    core, left = place_ref[0], place_ref[1].astype(F32)
    for own, ref in ((core, mine_ref), (1 - core, theirs_ref)):
        lay_out(
            own, left, ref.at[pl.ds(2 * block, cells)], ref.at[pl.ds(2 * block + cells, halo)], slab_ref
        )
    convolve(
        share, lambda p: place_ref[2 + p], lambda i: place_ref[2 + len(planes) + i],
        slab_ref, planes, conv_ref, pad_ref, low_ref, high_ref,
    )


def activate(cells, gain):
    cells = cells.astype(F32)
    scale = lax.rsqrt(jnp.mean(cells * cells, axis=-1, keepdims=True) + EPS)
    return jax.nn.silu(cells * scale * gain).astype(BF)


def three_parts(total):
    high = lax.reduce_precision(total, 8, 7)
    mid = lax.reduce_precision(total - high, 8, 7)
    return jnp.stack([high, mid, (total - high) - mid]).astype(BF)


def ring(data, axis, by):
    count = lax.axis_size(axis)
    return lax.ppermute(data, axis, [(i, (i + by) % count) for i in range(count)])


def swap(data, axis, bit):
    return lax.ppermute(data, axis, [(i, i ^ bit) for i in range(lax.axis_size(axis))])


def planes_of(data):
    count = lax.axis_size(X)
    return ring(data, X, 1), ring(data, X, count - 1), ring(data, X, 2)


def exchange(data, axes):
    return lax.all_to_all(data, axes, split_axis=0, concat_axis=0, tiled=True)


def shards(
    queries, keys, values, q_gain, k_gain, clip_ids, features, frame_cache, feat_gain, conv_weight
):
    tok, local_cols = queries.shape
    heads = local_cols // HEAD_DIM
    planes = lax.axis_size(X)
    plane_tok = heads * tok
    deep, cores = lax.axis_size("z"), lax.axis_size("core")
    seq_count = planes * deep * cores
    me_x, me_core = lax.axis_index(X), lax.axis_index("core")
    me_grp, me_rep = lax.axis_index("grp"), lax.axis_index("rep")
    parts = lax.axis_size("rep")
    order = jnp.stack([me_x, me_x - 1, me_x + 1, me_x + 2]) % planes

    q_f, k_f = queries.astype(F32), keys.astype(F32)
    sums = jnp.stack([jnp.sum(q_f * q_f, axis=-1), jnp.sum(k_f * k_f, axis=-1)])
    lanes = 128
    frames, tile_rows, tile_cols, _ = features.shape
    is_left, is_upper = me_grp == 0, me_core == 0
    raw_edge = jnp.concatenate(
        [
            jnp.where(is_left, frame_cache[:, :, -1], frame_cache[:, :, 0]),
            jnp.where(is_left, features[:, :, -1], features[:, :, 0]),
        ]
    )
    edge_count = raw_edge.shape[0] * raw_edge.shape[1]
    first_out = jnp.concatenate(
        [
            jnp.pad(three_parts(sums).reshape(6, tok), ((0, 0), (0, lanes - tok))),
            raw_edge.reshape(-1, lanes),
        ]
    )
    first_in = ring(first_out, "grp", 1)
    theirs = first_in[:6, :tok].astype(F32).reshape(3, 2, tok)
    sums = sums + ((theirs[0] + theirs[1]) + theirs[2])
    beside = first_in[6:].reshape(edge_count, CH)

    share = CH // parts
    weight_rows = conv_weight.shape[0]
    first = (me_rep + 2 * me_core) % parts
    held = jnp.arange(48)[:, None]
    late = (me_core == 1) & (me_rep >= 2)
    source = jnp.where(
        held < 40,
        4 * (held + late.astype(jnp.int32)) + first,
        jnp.where((held == 40) & (first < 2), jnp.where(me_core == 1, first, 160 + first), -1),
    )
    pick = (source == jnp.arange(weight_rows)[None, :]).astype(BF)
    chosen = jnp.dot(pick, conv_weight, preferred_element_type=F32).astype(BF)
    halves = chosen.reshape(48, cores, CH // cores).transpose(1, 0, 2)
    last = halves[:, :, 128:]
    halves = jnp.concatenate(
        [halves[:, :, :128], jnp.concatenate([last[:, :24], last[:, 24:]], axis=2)], axis=1
    )
    sent_weight = jnp.broadcast_to(halves[None], (deep,) + halves.shape).reshape(-1, 72, 128)
    plane_weight = exchange(sent_weight, ("z", "core"))

    scales = lax.rsqrt(sums / WIDTH + EPS)
    q_norm = (q_f * scales[0][:, None] * q_gain).astype(BF)
    k_norm = (k_f * scales[1][:, None] * k_gain).astype(BF)
    id_row = jnp.pad(clip_ids.astype(BF)[None, :], ((0, 7), (0, HEAD_DIM - tok)))

    def by_head(data):
        return data.reshape(tok, heads, HEAD_DIM).transpose(1, 0, 2)

    payload = jnp.concatenate(
        [
            by_head(q_norm),
            by_head(k_norm),
            by_head(values),
            jnp.broadcast_to(id_row[None], (heads,) + id_row.shape),
        ],
        axis=1,
    )
    got = exchange(payload, HEAD_AXES)
    slot = jnp.arange(deep * cores * 48)
    spot, item = slot // 48, slot % 48
    target = 81 * (spot // cores) + jnp.where(item == 40, 40, item + 41 * (spot % cores))
    target = jnp.where(item > 40, -1, target + (648 * me_x) % share)
    place = (jnp.arange(SLOTS * share)[:, None] == target[None, :]).astype(BF)
    place = place.reshape(SLOTS * share, deep * cores, 48)
    main = plane_weight[:, :48, :]
    rest = plane_weight[:, 48:, :]

    def placed_rows(at, data):
        return lax.dot_general(
            at, data, (((1, 2), (0, 1)), ((), ())), preferred_element_type=F32
        ).astype(BF)

    last_cols = (
        placed_rows(place[:, :, :24], rest)[:, :64] + placed_rows(place[:, :, 24:], rest)[:, 64:]
    )
    split = SLOTS * share // 2
    my_weight = jnp.concatenate(
        [
            placed_rows(place, main),
            jnp.concatenate([last_cols[:split], last_cols[split:]], axis=1),
        ],
        axis=0,
    )
    weights = (my_weight,) + planes_of(my_weight)
    taps = (27 * order) // planes
    got, after = lax.optimization_barrier((got, weights[2]))
    weights = weights[:2] + (after, weights[3])

    feat_f = features.astype(F32)
    stacked = jnp.concatenate([frame_cache, activate(features, feat_gain)], axis=0)
    lane = jnp.arange(parts * lanes)
    chan = jnp.where(
        lane % lanes < share, parts * (lane % lanes) + (me_rep + lane // lanes) % parts, -1
    )
    sort = (jnp.arange(CH)[:, None] == chan[None, :]).astype(BF)

    def by_class(data):
        data = jnp.dot(data, sort, preferred_element_type=F32).astype(BF)
        return data.reshape(-1, parts, lanes).transpose(1, 0, 2)

    beside = jnp.concatenate([beside[:-2], activate(beside[-2:], feat_gain)])
    beside = jnp.pad(beside, ((0, 16 - edge_count), (0, 0)))
    outgoing = jnp.concatenate([by_class(stacked.reshape(-1, CH)), by_class(beside)], axis=1)
    cells = jnp.stack([outgoing[0]] + [ring(outgoing[by], "rep", by) for by in range(1, parts)])
    main = cells[:, : 6 * tile_cols].reshape(parts, 3, tile_rows, tile_cols, lanes)
    ends = cells[:, 6 * tile_cols : 6 * tile_cols + 6].reshape(parts, 3, tile_rows, lanes)
    outer = jnp.where(is_upper, main[:, :, 0], main[:, :, -1]).reshape(parts, -1, lanes)
    outer_ends = jnp.where(is_upper, ends[:, :, 0], ends[:, :, -1])
    outer = jnp.concatenate([outer, jnp.pad(outer_ends, ((0, 0), (0, 13), (0, 0)))], axis=1)
    steps = [(s, s - 1 if s % 2 == 0 else s + 1) for s in range(1, seq_count - 1)]
    beyond = lax.ppermute(outer, SEQ, steps)

    ids_got = got[:, 3 * tok, :tok].reshape(-1)
    id_block = jnp.pad(ids_got.reshape(-1, HEAD_DIM), ((0, 16 - plane_tok // HEAD_DIM), (0, 0)))
    key_vals = jnp.concatenate(
        [got[:, tok : 3 * tok, :].reshape(2 * plane_tok, HEAD_DIM), id_block], axis=0
    )

    cells, beyond = cells.reshape(-1, lanes), beyond.reshape(-1, lanes)
    across = ring(key_vals, "xh", 1)
    across, *weights = lax.optimization_barrier((across,) + weights)
    mine = jnp.concatenate([key_vals, across, cells, beyond])
    theirs = ring(mine, "core", 1)
    sizes = key_vals.shape[0], cells.shape[0], beyond.shape[0]
    chip_cells = cores * tile_rows * tile_cols
    spots = me_rep ^ ((me_rep - jnp.arange(parts)) % parts)
    place = jnp.concatenate([jnp.stack([me_core, me_grp]), taps, spots]).astype(jnp.int32)
    head_out = pl.pallas_call(
        functools.partial(attention_kernel, tok, sizes[0]),
        out_shape=jax.ShapeDtypeStruct((plane_tok, HEAD_DIM), BF),
        in_specs=[VMEM] * 4,
        out_specs=VMEM,
        compiler_params=pltpu.CompilerParams(vmem_limit_bytes=40 << 20),
        cost_estimate=pl.CostEstimate(
            flops=4 * plane_tok * plane_tok * planes * HEAD_DIM,
            bytes_accessed=planes * plane_tok * HEAD_DIM * 4,
            transcendentals=plane_tok * plane_tok * planes,
        ),
        name="attention",
    )(got, mine, theirs, ids_got.astype(F32)[:, None])
    place, head_out = lax.optimization_barrier((place, head_out))
    partial = pl.pallas_call(
        functools.partial(conv_kernel, share, sizes),
        out_shape=jax.ShapeDtypeStruct((parts, chip_cells + chip_cells // 2, 128), BF),
        in_specs=[pl.BlockSpec(memory_space=pltpu.SMEM)] + [VMEM] * (2 + len(weights)),
        out_specs=VMEM,
        scratch_shapes=[
            pltpu.VMEM((3, parts, 3, cores * tile_rows + 2, tile_cols, lanes), BF),
            pltpu.VMEM((SLOTS, lanes, 256), BF),
            pltpu.VMEM((parts, chip_cells, 256), F32),
            pltpu.VMEM((parts, chip_cells, 256), F32),
        ],
        compiler_params=pltpu.CompilerParams(vmem_limit_bytes=48 << 20),
        cost_estimate=pl.CostEstimate(
            flops=2 * parts * chip_cells * 32 * lanes * 256,
            bytes_accessed=27 * lanes * CH,
            transcendentals=0,
        ),
        name="convolution",
    )(place, mine, theirs, *weights)
    returned = exchange(head_out.reshape(heads, tok, HEAD_DIM), HEAD_AXES)

    from_two = swap(partial[2:], "rep", 2)
    sums_back = partial[:2].astype(F32) + from_two.astype(F32)
    sums_back = sums_back[0] + swap(sums_back[1].astype(BF), "rep", 1).astype(F32)
    tile_cells = tile_rows * tile_cols
    main_cols = sums_back[:chip_cells].reshape(cores, tile_cells, 128)
    last_cols = sums_back[chip_cells:].reshape(tile_cells, cores, 64).transpose(1, 0, 2)
    both = jnp.concatenate([main_cols, last_cols], axis=2)
    keep = jnp.where(is_upper, both[0], both[1])
    give = jnp.where(is_upper, both[1], both[0]).astype(BF)
    take = ring(give, "core", 1).astype(F32)
    convolved = jnp.where(
        is_upper,
        jnp.concatenate([keep, take], axis=1),
        jnp.concatenate([take, keep], axis=1),
    ).reshape(features.shape)
    attended = returned.transpose(1, 0, 2).reshape(tok, local_cols)
    decoded = (feat_f + convolved).astype(BF)
    return (attended, decoded)


def solution(mesh):
    grid = Mesh(
        mesh.devices.reshape((2, 2, 8, 2) + mesh.devices.shape[1:]),
        ("xh", "xl", "z", "core", "grp", "rep"),
    )
    tokens = P(("rep",) + SEQ, "grp")
    image = P("rep", SEQ, "grp", None)
    placed = (
        tokens,
        tokens,
        tokens,
        P("grp"),
        P("grp"),
        P(("rep",) + SEQ),
        image,
        image,
        P(),
        P(SEQ, None),
    )
    return jax.shard_map(
        shards, mesh=grid, in_specs=placed, out_specs=(tokens, image), check_vma=False
    )
```
